128 devices in a mesh: grp: 8 (over x, core), sub: 16 (over z, y).
Axes of the slice: x: 4, y: 4, z: 4, core: 2. Of those that a mesh axis runs over, the one named last changes fastest.
Arguments:
- bg_vel: float32 [3, 64, 256, 256], P(None, 'grp', 'sub'), may hold values from -6 to 6
- nb_vel: float32 [3, 64, 256, 256], P(None, 'grp', 'sub'), may hold values from -6 to 6
- bg_source: float32 [3, 64, 256, 256], P(None, 'grp', 'sub'), may hold values from -6 to 6
- nb_source: float32 [3, 64, 256, 256], P(None, 'grp', 'sub'), may hold values from -6 to 6
- bg_inertia: float32 [64, 256, 256], P('grp', 'sub'), may hold values from 0.5 to 4
- nb_inertia: float32 [64, 256, 256], P('grp', 'sub'), may hold values from 0.5 to 4
- bg_donor_cells: int32 [128, 128, 128], P(('grp', 'sub')), may hold values from 0 to 28414, as said below
- bg_donor_weights: float32 [128, 128, 8, 128], P(('grp', 'sub')), may hold values from 0 to 1, as said below
- nb_donor_cells: int32 [128, 128, 128], P(('grp', 'sub')), may hold values from 0 to 28414, as said below
- nb_donor_weights: float32 [128, 128, 8, 128], P(('grp', 'sub')), may hold values from 0 to 1, as said below
- nb_receptors: int32 [128, 128, 128], P(('grp', 'sub')), may hold values from -1 to 30719, as said below
- bg_receptors: int32 [128, 128, 128], P(('grp', 'sub')), may hold values from -1 to 30719, as said below
Outputs:
- bg_out: float32 [3, 64, 256, 256], P(None, 'grp', 'sub')
- nb_out: float32 [3, 64, 256, 256], P(None, 'grp', 'sub')
The draws below stay inside these ranges and needn't reach their ends.
Inputs may be any that keep to these rules, and one draw needn't show every extreme that they name: `bg_donor_cells`: every base cell has streamwise, spanwise and vertical coordinates below 7, 15 and 255, so that its eight corners lie in the donor's block. `nb_donor_cells`: as for bg_donor_cells. `bg_donor_weights`: the eight weights of a slot are non-negative and sum to one. `nb_donor_weights`: as for bg_donor_weights. `nb_receptors`: live entries are flat cell indices into the receiving device's block. The live cells of one receiving device are distinct; for each donor device the live slots come first and number at least 32; on every receiving device some donor device fills all 128 slots. `bg_receptors`: as for nb_receptors.
All inputs are finite; a program needn't handle non-finite values.
Results may differ from the reference program's by a relative error of at most 0.0003.
Values sent between devices are 32-bit elements; how exact they have to be, the bound alone decides.
A program may use at most 256 MiB of HBM per device.

```python
import math
import jax
import jax.numpy as jnp
from jax import lax

CX = 8
CY = 16
CZ = 256
CAP = 128
SWEEPS = 4
SOURCES = 128
NX = 64
NY = 256
LIVE_CELLS = 30720
N_GRP = 8
N_SUB = 16


def donor_bases(key):
    first_key, second_key, third_key = jax.random.split(key, 3)
    shape = (SOURCES, SOURCES, CAP)
    coord_x = jax.random.randint(first_key, shape, 0, CX - 1)
    coord_y = jax.random.randint(second_key, shape, 0, CY - 1)
    coord_z = jax.random.randint(third_key, shape, 0, CZ - 1)
    cells = coord_x * (CY * CZ) + coord_y * CZ + coord_z
    top_cell = (CX - 2) * CY * CZ + (CY - 2) * CZ + CZ - 2
    return cells.at[0, 0, 0].set(top_cell).astype(jnp.int32)


def trilinear(fraction):
    corners = []
    for step_x in (0, 1):
        for step_y in (0, 1):
            for step_z in (0, 1):
                weight_x = fraction[:, :, 0] if step_x else 1.0 - fraction[:, :, 0]
                weight_y = fraction[:, :, 1] if step_y else 1.0 - fraction[:, :, 1]
                weight_z = fraction[:, :, 2] if step_z else 1.0 - fraction[:, :, 2]
                corners.append(weight_x * weight_y * weight_z)
    return jnp.stack(corners, axis=2).astype(jnp.float32)


def receptor_row(row_key):
    order = jax.random.permutation(row_key, LIVE_CELLS).astype(jnp.int32)
    top_place = jnp.argmax(order == LIVE_CELLS - 1)
    first_value = order[0]
    order = order.at[top_place].set(first_value).at[0].set(LIVE_CELLS - 1)
    return order[:SOURCES * CAP]


def receptor_cells(key):
    first_key, second_key, third_key = jax.random.split(key, 3)
    row_keys = jax.random.split(first_key, SOURCES)
    cells = jax.vmap(receptor_row)(row_keys)
    cells = cells.reshape(SOURCES, SOURCES, CAP)
    counts = jax.random.randint(second_key, (SOURCES, SOURCES), max(1, CAP // 4), CAP + 1)
    full_source = jax.random.randint(third_key, (SOURCES,), 0, SOURCES)
    counts = jnp.where(jnp.arange(SOURCES)[None, :] == full_source[:, None], CAP, counts)
    slots = jnp.arange(CAP)
    return jnp.where(slots[None, None, :] < counts[:, :, None], cells, -1).astype(jnp.int32)


def draw_bg_donor_cells(key, part):
    key = jax.random.fold_in(key, 11)
    return donor_bases(key)


def draw_nb_donor_cells(key, part):
    key = jax.random.fold_in(key, 12)
    return donor_bases(key)


def draw_bg_donor_weights(key, part):
    key = jax.random.fold_in(key, 13)
    fraction = jax.random.uniform(key, (SOURCES, SOURCES, 3, CAP), jnp.float32)
    return trilinear(fraction)


def draw_nb_donor_weights(key, part):
    key = jax.random.fold_in(key, 14)
    fraction = jax.random.uniform(key, (SOURCES, SOURCES, 3, CAP), jnp.float32)
    return trilinear(fraction)


def draw_nb_receptors(key, part):
    key = jax.random.fold_in(key, 15)
    return receptor_cells(key)


def draw_bg_receptors(key, part):
    key = jax.random.fold_in(key, 16)
    return receptor_cells(key)


def block_levels(own_key, shape, cuts, smallest, high):
    def one(axis_at, blocks):
        draws = jax.random.uniform(jax.random.fold_in(jax.random.fold_in(own_key, 6), axis_at), (blocks,), jnp.float32, smallest / len(cuts), high / len(cuts))
        return jnp.repeat(jnp.exp(draws), shape[axis_at] // blocks).reshape((-1,) + (1,) * (len(shape) - axis_at - 1))

    gain = one(*cuts[0])
    for cut in cuts[1:]:
        gain = gain * one(*cut)
    return gain


def gaussian(rng, dims, width, bound, pieces=(), kind=jnp.bfloat16):
    values = jax.random.normal(rng, dims, jnp.float32) * width
    if len(pieces) > 0:
        values = block_levels(rng, dims, pieces, -0.22, 0.18) * values
    return jnp.clip(values, min=-bound, max=bound).astype(kind)


def setup_inputs(seed: int = 0) -> dict:
    splits = jax.random.split(jax.random.key(seed), 13)
    bg_vel = gaussian(splits[0], (3, NX, NY, CZ), 1.0, 6.0, ((1, 8), (2, 16)), jnp.float32)
    nb_vel = gaussian(splits[1], (3, NX, NY, CZ), 1.0, 6.0, ((1, 8), (2, 16)), jnp.float32)
    bg_source = gaussian(splits[2], (3, NX, NY, CZ), 1.0, 6.0, ((1, 8), (2, 16)), jnp.float32)
    nb_source = gaussian(splits[3], (3, NX, NY, CZ), 1.0, 6.0, ((1, 8), (2, 16)), jnp.float32)
    bg_inertia = jnp.clip(jnp.exp(math.log(4.0) - 2.0794415 * jax.random.uniform(splits[4], (NX, NY, CZ), jnp.float32) ** block_levels(splits[4], (NX, NY, CZ), ((0, 8), (1, 16)), -0.2, 0.2)), 0.5, 4.0)
    nb_inertia = jnp.clip(jnp.exp(math.log(4.0) - 2.0794415 * jax.random.uniform(splits[5], (NX, NY, CZ), jnp.float32) ** block_levels(splits[5], (NX, NY, CZ), ((0, 8), (1, 16)), -0.2, 0.2)), 0.5, 4.0)
    bg_donor_cells = draw_bg_donor_cells(jax.random.fold_in(splits[12], 71), 0)
    bg_donor_weights = draw_bg_donor_weights(jax.random.fold_in(splits[12], 71), 0)
    nb_donor_cells = draw_nb_donor_cells(jax.random.fold_in(splits[12], 71), 0)
    nb_donor_weights = draw_nb_donor_weights(jax.random.fold_in(splits[12], 71), 0)
    nb_receptors = draw_nb_receptors(jax.random.fold_in(splits[12], 71), 0)
    bg_receptors = draw_bg_receptors(jax.random.fold_in(splits[12], 71), 0)
    return {"bg_vel": bg_vel, "nb_vel": nb_vel, "bg_source": bg_source, "nb_source": nb_source, "bg_inertia": bg_inertia, "nb_inertia": nb_inertia, "bg_donor_cells": bg_donor_cells, "bg_donor_weights": bg_donor_weights, "nb_donor_cells": nb_donor_cells, "nb_donor_weights": nb_donor_weights, "nb_receptors": nb_receptors, "bg_receptors": bg_receptors}


def stencil_offsets(rows_y, rows_z):
    return jnp.array([step_x * rows_y * rows_z + step_y * rows_z + step_z for step_x in (0, 1) for step_y in (0, 1) for step_z in (0, 1)], jnp.int32)


def interpolate(flat_field, base_cells, weights, offsets_table):
    indices = base_cells[:, None, :] + offsets_table[None, :, None]
    values = flat_field[:, indices]
    return jnp.sum(values * weights[None], axis=2)


def overwrite(flat_field, receptors, values):
    cells_total = flat_field.shape[1]
    indices = jnp.where(receptors < 0, cells_total, receptors).reshape(-1)
    updated = flat_field.at[:, indices].set(values.reshape(values.shape[0], -1), mode="drop")
    frozen = jnp.zeros((1, cells_total), jnp.float32).at[:, indices].set(1.0, mode="drop")
    return updated, frozen


def cell_faces(padded):
    middle = padded[..., 1:-1, 1:-1, 1:-1]
    after_cells = (padded[..., 2:, 1:-1, 1:-1], padded[..., 1:-1, 2:, 1:-1], padded[..., 1:-1, 1:-1, 2:])
    before_cells = (padded[..., :-2, 1:-1, 1:-1], padded[..., 1:-1, :-2, 1:-1], padded[..., 1:-1, 1:-1, :-2])
    return middle, after_cells, before_cells


def assemble(padded, inertia):
    middle, after_cells, before_cells = cell_faces(padded)
    coef_after = tuple(1.0 + jax.nn.relu(-0.5 * (middle[direction] + after_cells[direction][direction])) for direction in range(3))
    coef_before = tuple(1.0 + jax.nn.relu(0.5 * (middle[direction] + before_cells[direction][direction])) for direction in range(3))
    diagonal = inertia
    for direction in range(3):
        diagonal = diagonal + coef_after[direction] + coef_before[direction]
    return coef_after, coef_before, diagonal


def relax(padded, coef_after, coef_before, diagonal, right_side, frozen):
    middle, after_cells, before_cells = cell_faces(padded)
    summed = right_side
    for direction in range(3):
        summed = summed + coef_after[direction] * after_cells[direction] + coef_before[direction] * before_cells[direction]
    return jnp.where(frozen, middle, summed / diagonal)


def pad_cells(velocity):
    widths = [(0, 0)] * (velocity.ndim - 3) + [(1, 1)] * 3
    return jnp.pad(velocity, widths)


def solve_grid(start, source, inertia, frozen):
    padded = pad_cells(start)
    coef_after, coef_before, diagonal = assemble(padded, inertia)
    right_side = source + inertia * start
    velocity = start
    for sweep_index in range(SWEEPS):
        if sweep_index > 0:
            padded = pad_cells(velocity)
        velocity = relax(padded, coef_after, coef_before, diagonal, right_side, frozen)
    return velocity


def to_blocks(velocity):
    comps = velocity.shape[0]
    shaped = velocity.reshape(comps, N_GRP, CX, N_SUB, CY, CZ)
    return shaped.transpose(1, 3, 0, 2, 4, 5).reshape(N_GRP * N_SUB, comps, CX * CY * CZ)


def from_blocks(flat_blocks):
    comps = flat_blocks.shape[1]
    shaped = flat_blocks.reshape(N_GRP, N_SUB, comps, CX, CY, CZ)
    return shaped.transpose(2, 0, 3, 1, 4, 5).reshape(comps, N_GRP * CX, N_SUB * CY, CZ)


def reference(bg_vel, nb_vel, bg_source, nb_source, bg_inertia, nb_inertia, bg_donor_cells, bg_donor_weights, nb_donor_cells, nb_donor_weights, nb_receptors, bg_receptors):
    offsets_table = stencil_offsets(CY, CZ)
    bg_blocks = to_blocks(bg_vel)
    nb_blocks = to_blocks(nb_vel)

    def from_donor(donor_tuple):
        return interpolate(donor_tuple[0], donor_tuple[1], donor_tuple[2], offsets_table)

    to_near = lax.map(from_donor, (bg_blocks, bg_donor_cells, bg_donor_weights))
    to_near = jnp.transpose(to_near, (2, 1, 0, 3))
    to_back = lax.map(from_donor, (nb_blocks, nb_donor_cells, nb_donor_weights))
    to_back = jnp.transpose(to_back, (2, 1, 0, 3))
    nb_blocks, nb_mask = jax.vmap(overwrite)(nb_blocks, nb_receptors, to_near)
    bg_blocks, bg_mask = jax.vmap(overwrite)(bg_blocks, bg_receptors, to_back)
    bg_start = from_blocks(bg_blocks)
    bg_frozen = from_blocks(bg_mask)[0] > 0.5
    nb_start = from_blocks(nb_blocks)
    nb_frozen = from_blocks(nb_mask)[0] > 0.5
    bg_out = solve_grid(bg_start, bg_source, bg_inertia, bg_frozen)
    block_shape = (3, N_GRP, CX, N_SUB * CY, CZ)
    nb_out = solve_grid(nb_start.reshape(block_shape), nb_source.reshape(block_shape), nb_inertia.reshape(block_shape[1:]), nb_frozen.reshape(block_shape[1:]))
    return bg_out, nb_out.reshape(nb_vel.shape)
```

```python
import jax
import jax.numpy as jnp
from jax import lax
from jax.experimental import pallas as pl
from jax.experimental.pallas import tpu as pltpu
from jax.sharding import PartitionSpec as P

BF = jnp.bfloat16
F32 = jnp.float32


def split(x):
    hi = x.astype(BF)
    lo = (x - hi.astype(F32)).astype(BF)
    return hi, lo


def interp_one(field, cells, weights, out, table, base):
    x = field[...].reshape(384, 256)
    hi, lo = split(x)
    table[0:384, :] = hi
    table[768:1152, :] = lo
    hi, lo = split(pltpu.roll(x, 255, 1))
    table[384:768, :] = hi
    table[1152:1536, :] = lo
    z_iota = lax.broadcasted_iota(jnp.int32, (256, 128), 0).astype(F32).astype(BF)
    y_iota = lax.broadcasted_iota(jnp.int32, (16, 128), 0)

    def step(i, carry):
        tile = cells[0, pl.ds(pl.multiple_of(i * 8, 8), 8), :]
        z_tile = (tile & 255).astype(F32).astype(BF)
        y_tile = (tile >> 8) & 15
        x_tile = tile >> 12
        for pair in range(4):
            hot = [
                jnp.where(z_iota == z_tile[s : s + 1, :], jnp.ones((), BF), jnp.zeros((), BF))
                for s in (2 * pair, 2 * pair + 1)
            ]
            hot = jnp.concatenate(hot, axis=1)
            got = jnp.dot(table[0:768, :], hot, preferred_element_type=F32)
            got = got + jnp.dot(table[768:1536, :], hot, preferred_element_type=F32)
            for half in range(2):
                s = 2 * pair + half
                r = i * 8 + s
                w = weights[0, r]
                y_row = y_tile[s : s + 1, :]
                x_row = jnp.broadcast_to(x_tile[s : s + 1, :], (16, 128))
                y_here = y_iota == y_row
                y_next = y_iota == y_row + 1
                by_y = {}
                for a in range(2):
                    for zc in range(2):
                        k = 4 * a + zc
                        by_y[a, zc] = jnp.where(
                            y_here, w[k : k + 1, :], jnp.where(y_next, w[k + 2 : k + 3, :], 0.0)
                        )
                acc = [None] * 3
                before = None
                for xx in range(8):
                    here = x_row == xx if xx < 7 else None
                    for zc in range(2):
                        coef = None
                        if before is not None:
                            coef = jnp.where(before, by_y[1, zc], 0.0)
                        if here is not None:
                            coef = jnp.where(here, by_y[0, zc], 0.0 if coef is None else coef)
                        for c in range(3):
                            at = zc * 384 + c * 128 + xx * 16
                            term = coef * got[at : at + 16, half * 128 : half * 128 + 128]
                            acc[c] = term if acc[c] is None else acc[c] + term
                    before = here
                for c in range(3):
                    out[r, base + c, :] = jnp.sum(acc[c], axis=0)
        return carry

    lax.fori_loop(0, 16, step, 0)


def interp_kernel(bg_vel, bg_cells, bg_w, nb_vel, nb_cells, nb_w, out, table):
    interp_one(bg_vel, bg_cells, bg_w, out, table, 0)
    interp_one(nb_vel, nb_cells, nb_w, out, table, 3)


def interpolate(*args):
    return pl.pallas_call(
        interp_kernel,
        out_shape=jax.ShapeDtypeStruct((128, 8, 128), F32),
        in_specs=[pl.BlockSpec(memory_space=pltpu.VMEM)] * 6,
        out_specs=pl.BlockSpec(memory_space=pltpu.VMEM),
        scratch_shapes=[pltpu.VMEM((1536, 256), BF)],
        compiler_params=pltpu.CompilerParams(vmem_limit_bytes=40 * 2**20),
        name="interpolate",
    )(*args)


def scatter_one(field, receptors, got, base, start, frozen, left, total):
    z_iota = lax.broadcasted_iota(jnp.int32, (256, 128), 0).astype(F32).astype(BF)
    r_iota = lax.broadcasted_iota(jnp.int32, (128, 128), 0).astype(F32).astype(BF)
    one = jnp.ones((), BF)
    zero = jnp.zeros((), BF)
    total[...] = jnp.zeros_like(total)

    def step(i, carry):
        tile = receptors[0, pl.ds(pl.multiple_of(i * 8, 8), 8), :]
        z_tile = (tile & 255).astype(F32).astype(BF)
        r_tile = (tile >> 8).astype(F32).astype(BF)
        hots = []
        for s in range(8):
            hots.append(jnp.where(z_iota == z_tile[s : s + 1, :], one, zero))
            mine = r_iota == r_tile[s : s + 1, :]
            values = got[i * 8 + s]
            hi, lo = split(values)
            for c in range(3):
                left[c * 128 : c * 128 + 128, s * 128 : s * 128 + 128] = jnp.where(
                    mine, hi[base + c : base + c + 1, :], zero
                )
                left[384 + c * 128 : 512 + c * 128, s * 128 : s * 128 + 128] = jnp.where(
                    mine, lo[base + c : base + c + 1, :], zero
                )
            left[768:896, s * 128 : s * 128 + 128] = jnp.where(mine, one, zero)
        hot = jnp.concatenate(hots, axis=1)
        total[...] += lax.dot_general(
            left[...], hot, (((1,), (1,)), ((), ())), preferred_element_type=F32
        )
        return carry

    lax.fori_loop(0, 16, step, 0)
    mask = total[768:896, :]
    frozen[...] = mask.reshape(8, 16, 256)
    for c in range(3):
        value = total[c * 128 : c * 128 + 128, :] + total[384 + c * 128 : 512 + c * 128, :]
        old = field[c].reshape(128, 256)
        start[c] = jnp.where(mask > 0.5, value, old).reshape(8, 16, 256)


def scatter_kernel(
    got, nb_rec, bg_rec, nb_vel, bg_vel, nb_start, nb_frozen, bg_start, bg_frozen, left, total
):
    scatter_one(nb_vel, nb_rec, got, 0, nb_start, nb_frozen, left, total)
    scatter_one(bg_vel, bg_rec, got, 3, bg_start, bg_frozen, left, total)


def overwrite(*args):
    field = jax.ShapeDtypeStruct((3, 8, 16, 256), F32)
    mask = jax.ShapeDtypeStruct((8, 16, 256), F32)
    return pl.pallas_call(
        scatter_kernel,
        out_shape=(field, mask, field, mask),
        in_specs=[pl.BlockSpec(memory_space=pltpu.VMEM)] * 5,
        out_specs=[pl.BlockSpec(memory_space=pltpu.VMEM)] * 4,
        scratch_shapes=[pltpu.VMEM((896, 1024), BF), pltpu.VMEM((896, 256), F32)],
        compiler_params=pltpu.CompilerParams(vmem_limit_bytes=40 * 2**20),
        name="overwrite",
    )(*args)


SWEEPS = 4


def extended(block, sides, width):
    for axis, dim in sides:
        count = lax.axis_size(axis)
        forward = [(i, i + 1) for i in range(count - 1)]
        backward = [(target, source) for source, target in forward]
        low = lax.ppermute(
            lax.slice_in_dim(block, block.shape[dim] - width, None, axis=dim), axis, forward
        )
        high = lax.ppermute(lax.slice_in_dim(block, 0, width, axis=dim), axis, backward)
        block = jnp.concatenate([low, block, high], axis=dim)
    return block


def cell_faces(padded):
    middle = padded[..., 1:-1, 1:-1, 1:-1]
    after_cells = (
        padded[..., 2:, 1:-1, 1:-1],
        padded[..., 1:-1, 2:, 1:-1],
        padded[..., 1:-1, 1:-1, 2:],
    )
    before_cells = (
        padded[..., :-2, 1:-1, 1:-1],
        padded[..., 1:-1, :-2, 1:-1],
        padded[..., 1:-1, 1:-1, :-2],
    )
    return (middle, after_cells, before_cells)


def assemble(padded, inertia):
    middle, after_cells, before_cells = cell_faces(padded)
    coef_after = tuple(
        (
            1.0 + jax.nn.relu(-0.5 * (middle[direction] + after_cells[direction][direction]))
            for direction in range(3)
        )
    )
    coef_before = tuple(
        (
            1.0 + jax.nn.relu(0.5 * (middle[direction] + before_cells[direction][direction]))
            for direction in range(3)
        )
    )
    diagonal = inertia
    for direction in range(3):
        diagonal = diagonal + coef_after[direction] + coef_before[direction]
    return (coef_after, coef_before, diagonal)


def relax(padded, coef_after, coef_before, diagonal, right_side, frozen):
    middle, after_cells, before_cells = cell_faces(padded)
    summed = right_side
    for direction in range(3):
        summed = (
            summed
            + coef_after[direction] * after_cells[direction]
            + coef_before[direction] * before_cells[direction]
        )
    return jnp.where(frozen, middle, summed / diagonal)


def pad_background(velocity):
    padded = extended(velocity, (("grp", 1), ("sub", 2)), 1)
    return jnp.pad(padded, ((0, 0), (0, 0), (0, 0), (1, 1)))


def pad_nearbody(velocity):
    padded = extended(velocity, (("sub", 2),), 1)
    return jnp.pad(padded, ((0, 0), (1, 1), (0, 0), (1, 1)))


def solve_grid(start, source, inertia, frozen, padder):
    padded = padder(start)
    coef_after, coef_before, diagonal = assemble(padded, inertia)
    right_side = source + inertia * start
    velocity = start
    for sweep_index in range(SWEEPS):
        if sweep_index > 0:
            padded = padder(velocity)
        velocity = relax(padded, coef_after, coef_before, diagonal, right_side, frozen)
    return velocity


def body(
    bg_vel,
    nb_vel,
    bg_source,
    nb_source,
    bg_inertia,
    nb_inertia,
    bg_donor_cells,
    bg_donor_weights,
    nb_donor_cells,
    nb_donor_weights,
    nb_receptors,
    bg_receptors,
):
    sent = interpolate(bg_vel, bg_donor_cells, bg_donor_weights, nb_vel, nb_donor_cells, nb_donor_weights)
    got = lax.all_to_all(sent, ("grp", "sub"), split_axis=0, concat_axis=0, tiled=True)
    nb_start, nb_mask, bg_start, bg_mask = overwrite(got, nb_receptors, bg_receptors, nb_vel, bg_vel)
    bg_out = solve_grid(
        bg_start, bg_source, bg_inertia, bg_mask > 0.5, pad_background
    )
    nb_out = solve_grid(
        nb_start, nb_source, nb_inertia, nb_mask > 0.5, pad_nearbody
    )
    return (bg_out, nb_out)


def solution(mesh):
    return jax.shard_map(
        body,
        mesh=mesh,
        in_specs=(
            P(None, "grp", "sub", None),
            P(None, "grp", "sub", None),
            P(None, "grp", "sub", None),
            P(None, "grp", "sub", None),
            P("grp", "sub", None),
            P("grp", "sub", None),
            P(("grp", "sub"), None, None),
            P(("grp", "sub"), None, None, None),
            P(("grp", "sub"), None, None),
            P(("grp", "sub"), None, None, None),
            P(("grp", "sub"), None, None),
            P(("grp", "sub"), None, None),
        ),
        out_specs=(P(None, "grp", "sub", None), P(None, "grp", "sub", None)),
        check_vma=False,
    )
```

```python
import jax
import jax.numpy as jnp
from jax import lax
from jax.experimental import pallas as pl
from jax.experimental.pallas import tpu as pltpu
from jax.sharding import PartitionSpec as P

BF = jnp.bfloat16
F32 = jnp.float32
MESH = pl.DeviceIdType.MESH
SWEEPS = 4


def split(x):
    hi = x.astype(BF)
    lo = (x - hi.astype(F32)).astype(BF)
    return hi, lo


def place(device):
    return (device // 16, device % 16)


def iota(shape, dim):
    return lax.broadcasted_iota(jnp.int32, shape, dim)


def build_table(field, table):
    x = field[...].reshape(384, 256)
    hi, lo = split(x)
    table[0:384, :] = hi
    table[768:1152, :] = lo
    hi, lo = split(pltpu.roll(x, 255, 1))
    table[384:768, :] = hi
    table[1152:1536, :] = lo


def interpolate_tile(t, cells, weights, out, table):
    z_iota = iota((256, 128), 0).astype(F32).astype(BF)
    y_iota = iota((16, 128), 0)
    tile = cells[0, pl.ds(pl.multiple_of(t * 8, 8), 8), :]
    z_tile = (tile & 255).astype(F32).astype(BF)
    y_tile = (tile >> 8) & 15
    x_tile = tile >> 12
    for pair in range(4):
        hot = [
            jnp.where(z_iota == z_tile[s : s + 1, :], jnp.ones((), BF), jnp.zeros((), BF))
            for s in (2 * pair, 2 * pair + 1)
        ]
        hot = jnp.concatenate(hot, axis=1)
        got = jnp.dot(table[0:768, :], hot, preferred_element_type=F32)
        got = got + jnp.dot(table[768:1536, :], hot, preferred_element_type=F32)
        for half in range(2):
            s = 2 * pair + half
            r = t * 8 + s
            w = weights[0, r]
            y_row = y_tile[s : s + 1, :]
            x_row = jnp.broadcast_to(x_tile[s : s + 1, :], (16, 128))
            y_here = y_iota == y_row
            y_next = y_iota == y_row + 1
            by_y = {}
            for a in range(2):
                for zc in range(2):
                    k = 4 * a + zc
                    by_y[a, zc] = jnp.where(
                        y_here, w[k : k + 1, :], jnp.where(y_next, w[k + 2 : k + 3, :], 0.0)
                    )
            acc = [None] * 3
            before = None
            for xx in range(8):
                here = x_row == xx if xx < 7 else None
                for zc in range(2):
                    coef = None
                    if before is not None:
                        coef = jnp.where(before, by_y[1, zc], 0.0)
                    if here is not None:
                        coef = jnp.where(here, by_y[0, zc], 0.0 if coef is None else coef)
                    for c in range(3):
                        at = zc * 384 + c * 128 + xx * 16
                        term = coef * got[at : at + 16, half * 128 : half * 128 + 128]
                        acc[c] = term if acc[c] is None else acc[c] + term
                before = here
            for c in range(3):
                out[r, c, :] = jnp.sum(acc[c], axis=0)


def interpolate(field, cells, weights, sent, came, table, sems, me):
    build_table(field, table)
    mine = me // 8

    def send(target):
        pltpu.make_async_remote_copy(
            src_ref=sent.at[target],
            dst_ref=came.at[me],
            send_sem=sems.at[0],
            recv_sem=sems.at[1],
            device_id=place(target),
            device_id_type=MESH,
        ).start()

    def step(i, carry):
        t = (mine + 1 + i) % 16
        interpolate_tile(t, cells, weights, sent, table)

        @pl.when(i < 15)
        def _():
            for s in range(8):
                send(t * 8 + (me + s) % 8)

        return carry

    lax.fori_loop(0, 16, step, 0)
    for s in range(1, 8):
        send(mine * 8 + (me + s) % 8)
    came[me] = sent[me]


def all_of(sent, came, sems, me):
    return pltpu.make_async_remote_copy(
        src_ref=sent.at[pl.ds(0, 127)],
        dst_ref=came.at[pl.ds(0, 127)],
        send_sem=sems.at[0],
        recv_sem=sems.at[1],
        device_id=place((me + 1) % 128),
        device_id_type=MESH,
    )


def overwrite(field, receptors, got, start, frozen, left, total):
    z_iota = iota((256, 128), 0).astype(F32).astype(BF)
    r_iota = iota((128, 128), 0).astype(F32).astype(BF)
    one = jnp.ones((), BF)
    zero = jnp.zeros((), BF)
    total[...] = jnp.zeros_like(total)

    def step(i, carry):
        tile = receptors[0, pl.ds(pl.multiple_of(i * 8, 8), 8), :]
        z_tile = (tile & 255).astype(F32).astype(BF)
        r_tile = (tile >> 8).astype(F32).astype(BF)
        hots = []
        for s in range(8):
            hots.append(jnp.where(z_iota == z_tile[s : s + 1, :], one, zero))
            mine = r_iota == r_tile[s : s + 1, :]
            hi, lo = split(got[i * 8 + s])
            at = slice(s * 128, s * 128 + 128)
            for c in range(3):
                left[c * 128 : c * 128 + 128, at] = jnp.where(mine, hi[c : c + 1, :], zero)
                left[384 + c * 128 : 512 + c * 128, at] = jnp.where(mine, lo[c : c + 1, :], zero)
            left[768:896, at] = jnp.where(mine, one, zero)
        hot = jnp.concatenate(hots, axis=1)
        total[...] += lax.dot_general(
            left[...], hot, (((1,), (1,)), ((), ())), preferred_element_type=F32
        )
        return carry

    lax.fori_loop(0, 16, step, 0)
    mask = total[768:896, :]
    frozen[...] = mask.reshape(8, 16, 256)
    for c in range(3):
        value = total[c * 128 : c * 128 + 128, :] + total[384 + c * 128 : 512 + c * 128, :]
        old = field[c].reshape(128, 256)
        start[c, 1:9] = jnp.where(mask > 0.5, value, old).reshape(8, 16, 256)


def halo_copies(grid, k, velocity, edge, halo, send_sems, recv_sems, g, s):
    north, south = (s + 1) % 16, (s + 15) % 16
    plan = [
        (edge.at[grid, k, 0], halo.at[grid, k, 0], (g, north)),
        (edge.at[grid, k, 1], halo.at[grid, k, 1], (g, south)),
    ]
    if grid == 0:
        plan += [
            (velocity.at[k, :, 8], velocity.at[k, :, 0], ((g + 1) % 8, s)),
            (velocity.at[k, :, 1], velocity.at[k, :, 9], ((g + 7) % 8, s)),
        ]
    return [
        pltpu.make_async_remote_copy(
            src_ref=source,
            dst_ref=target,
            send_sem=send_sems.at[grid, k, n],
            recv_sem=recv_sems.at[grid, k, n],
            device_id=device,
            device_id_type=MESH,
        )
        for n, (source, target, device) in enumerate(plan)
    ]


def fill_edges(grid, k, velocity, edge):
    for c in range(3):
        edge[grid, k, 0, c] = velocity[k, c, 1:9, 15, :]
        edge[grid, k, 1, c] = velocity[k, c, 1:9, 0, :]


def shifted(plane, low, high):
    y = iota((16, 256), 0)
    after_y = jnp.where(y == 15, high, pltpu.roll(plane, 15, 0))
    before_y = jnp.where(y == 0, low, pltpu.roll(plane, 1, 0))
    return after_y, before_y, pltpu.roll(plane, 255, 1), pltpu.roll(plane, 1, 1)


def assemble(grid, velocity, halo, source, inertia, frozen, coef, rhs, g, s):
    y = iota((16, 256), 0)
    z = iota((16, 256), 1)
    y_low = jnp.where(s > 0, 1.0, 0.0)
    y_high = jnp.where(s < 15, 1.0, 0.0)

    def face(middle, other, sign):
        return 1.0 + jnp.maximum(sign * (middle + other), 0.0)

    def step(x, carry):
        u, v, w = (velocity[0, c, x + 1] for c in range(3))
        if grid == 0:
            x_low = jnp.where((x > 0) | (g > 0), 1.0, 0.0)
            x_high = jnp.where((x < 7) | (g < 7), 1.0, 0.0)
        else:
            x_low = jnp.where(x > 0, 1.0, 0.0)
            x_high = jnp.where(x < 7, 1.0, 0.0)
        low = halo[grid, 0, 0, 1, pl.ds(x, 1), :] * y_low
        high = halo[grid, 0, 1, 1, pl.ds(x, 1), :] * y_high
        v_after, v_before, _, _ = shifted(v, low, high)
        w_after = jnp.where(z == 255, 0.0, pltpu.roll(w, 255, 1))
        w_before = jnp.where(z == 0, 0.0, pltpu.roll(w, 1, 1))
        faces = [
            face(u, velocity[0, 0, x + 2] * x_high, -0.5),
            face(u, velocity[0, 0, x] * x_low, 0.5),
            face(v, v_after, -0.5),
            face(v, v_before, 0.5),
            face(w, w_after, -0.5),
            face(w, w_before, 0.5),
        ]
        weight = inertia[x]
        diagonal = weight
        for f in faces:
            diagonal = diagonal + f
        inverse = 1.0 / diagonal
        stuck = frozen[x] > 0.5
        live = jnp.where(stuck, 0.0, inverse)
        faces = [f * live for f in faces]
        coef[0, x] = faces[0] * x_high
        coef[1, x] = faces[1] * x_low
        coef[2, x] = jnp.where(y == 15, faces[2] * y_high, faces[2])
        coef[3, x] = jnp.where(y == 0, faces[3] * y_low, faces[3])
        coef[4, x] = jnp.where(z == 255, 0.0, faces[4])
        coef[5, x] = jnp.where(z == 0, 0.0, faces[5])
        for c, start in enumerate((u, v, w)):
            right = (source[c, x] + weight * start) * inverse
            rhs[c, x] = jnp.where(stuck, start, right)
        return carry

    lax.fori_loop(0, 8, step, 0)


def sweep(grid, k, velocity, halo, coef, rhs, write):
    def step(x, carry):
        for c in range(3):
            after_y, before_y, after_z, before_z = shifted(
                velocity[k, c, x + 1],
                halo[grid, k, 0, c, pl.ds(x, 1), :],
                halo[grid, k, 1, c, pl.ds(x, 1), :],
            )
            total = rhs[c, x]
            total = total + coef[0, x] * velocity[k, c, x + 2] + coef[1, x] * velocity[k, c, x]
            total = total + coef[2, x] * after_y + coef[3, x] * before_y
            total = total + coef[4, x] * after_z + coef[5, x] * before_z
            write(c, x, total)
        return carry

    lax.fori_loop(0, 8, step, 0)


def kernel(*refs):
    (
        bg_vel_hbm, nb_vel_hbm, bg_source_hbm, nb_source_hbm, bg_inertia_hbm, nb_inertia_hbm,
        bg_cells_hbm, bg_weights_hbm, nb_cells_hbm, nb_weights_hbm, nb_rec_hbm, bg_rec_hbm,
        bg_out, nb_out,
        bg_vel, nb_vel, bg_source, nb_source, bg_inertia, nb_inertia,
        bg_cells, bg_weights, nb_cells, nb_weights, nb_rec, bg_rec,
        table, left, total,
        bg_sent, nb_sent, to_near, to_back, bg_run, nb_run,
        bg_frozen, nb_frozen, bg_coef, nb_coef, bg_rhs, nb_rhs, edge, halo,
        load_sems, near_sems, back_sems, send_sems, recv_sems, store_sems,
    ) = refs
    g = lax.axis_index("grp")
    s = lax.axis_index("sub")
    me = g * 16 + s

    hbm = refs[:12]
    vmem = refs[14:26]
    loads = [
        pltpu.make_async_copy(hbm[n], vmem[n], load_sems.at[n]) for n in range(12)
    ]
    for n in (0, 6, 7, 1, 8, 9, 10, 11, 2, 3, 4, 5):
        loads[n].start()

    barrier = pltpu.get_barrier_semaphore()

    def greet(i, carry):
        pl.semaphore_signal(
            barrier, inc=1, device_id=place((me + i) % 128), device_id_type=MESH
        )
        return carry

    lax.fori_loop(1, 128, greet, 0)
    pl.semaphore_wait(barrier, 127)
    for k in range(SWEEPS):
        for c in range(3):
            nb_run[k, c, 0] = jnp.zeros((16, 256), F32)
            nb_run[k, c, 9] = jnp.zeros((16, 256), F32)

    for n in (0, 6, 7):
        loads[n].wait()
    interpolate(bg_vel, bg_cells, bg_weights, bg_sent, to_near, table, near_sems, me)
    for n in (1, 8, 9):
        loads[n].wait()
    interpolate(nb_vel, nb_cells, nb_weights, nb_sent, to_back, table, back_sems, me)
    for n in (10, 11, 2, 3, 4, 5):
        loads[n].wait()

    copies = []

    def exchange(grid, k, velocity):
        fill_edges(grid, k, velocity, edge)
        new = halo_copies(grid, k, velocity, edge, halo, send_sems, recv_sems, g, s)
        for copy in new:
            copy.start()
        copies.extend(new)
        return new

    near = all_of(bg_sent, to_near, near_sems, me)
    near.wait_recv()
    overwrite(nb_vel, nb_rec, to_near, nb_run.at[0], nb_frozen, left, total)
    nb_moving = exchange(1, 0, nb_run)
    back = all_of(nb_sent, to_back, back_sems, me)
    back.wait_recv()
    overwrite(bg_vel, bg_rec, to_back, bg_run.at[0], bg_frozen, left, total)
    bg_moving = exchange(0, 0, bg_run)

    for k in range(SWEEPS):
        for copy in nb_moving:
            copy.wait_recv()
        if k == 0:
            assemble(1, nb_run, halo, nb_source, nb_inertia, nb_frozen, nb_coef, nb_rhs, g, s)

        def nb_write(c, x, value):
            if k < SWEEPS - 1:
                nb_run[k + 1, c, x + 1] = value
            else:
                nb_out[c, x] = value

        sweep(1, k, nb_run, halo, nb_coef, nb_rhs, nb_write)
        if k < SWEEPS - 1:
            nb_moving = exchange(1, k + 1, nb_run)
        for copy in bg_moving:
            copy.wait_recv()
        if k == 0:
            assemble(0, bg_run, halo, bg_source, bg_inertia, bg_frozen, bg_coef, bg_rhs, g, s)

        def bg_write(c, x, value):
            if k < SWEEPS - 1:
                bg_run[k + 1, c, x + 1] = value
            else:
                bg_out[c, x] = value

        sweep(0, k, bg_run, halo, bg_coef, bg_rhs, bg_write)
        if k < SWEEPS - 1:
            bg_moving = exchange(0, k + 1, bg_run)

    near.wait_send()
    back.wait_send()
    for copy in copies:
        copy.wait_send()


def body(*args):
    out = jax.ShapeDtypeStruct((3, 8, 16, 256), F32)
    vmem = pltpu.VMEM
    return pl.pallas_call(
        kernel,
        out_shape=(out, out),
        in_specs=[pl.BlockSpec(memory_space=pl.ANY)] * 12,
        out_specs=[pl.BlockSpec(memory_space=vmem)] * 2,
        scratch_shapes=[vmem(a.shape, a.dtype) for a in args]
        + [
            vmem((1536, 256), BF),
            vmem((896, 1024), BF),
            vmem((896, 256), F32),
            vmem((128, 4, 128), F32),
            vmem((128, 4, 128), F32),
            vmem((128, 4, 128), F32),
            vmem((128, 4, 128), F32),
            vmem((SWEEPS, 3, 10, 16, 256), F32),
            vmem((SWEEPS, 3, 10, 16, 256), F32),
            vmem((8, 16, 256), F32),
            vmem((8, 16, 256), F32),
            vmem((6, 8, 16, 256), F32),
            vmem((6, 8, 16, 256), F32),
            vmem((3, 8, 16, 256), F32),
            vmem((3, 8, 16, 256), F32),
            vmem((2, SWEEPS, 2, 3, 8, 256), F32),
            vmem((2, SWEEPS, 2, 3, 8, 256), F32),
            pltpu.SemaphoreType.DMA((12,)),
            pltpu.SemaphoreType.DMA((2,)),
            pltpu.SemaphoreType.DMA((2,)),
            pltpu.SemaphoreType.DMA((2, SWEEPS, 4)),
            pltpu.SemaphoreType.DMA((2, SWEEPS, 4)),
            pltpu.SemaphoreType.DMA((2,)),
        ],
        compiler_params=pltpu.CompilerParams(
            collective_id=0, has_side_effects=True, vmem_limit_bytes=48 * 2**20
        ),
        name="overset",
    )(*args)


def solution(mesh):
    return jax.shard_map(
        body,
        mesh=mesh,
        in_specs=(
            P(None, "grp", "sub", None),
            P(None, "grp", "sub", None),
            P(None, "grp", "sub", None),
            P(None, "grp", "sub", None),
            P("grp", "sub", None),
            P("grp", "sub", None),
            P(("grp", "sub"), None, None),
            P(("grp", "sub"), None, None, None),
            P(("grp", "sub"), None, None),
            P(("grp", "sub"), None, None, None),
            P(("grp", "sub"), None, None),
            P(("grp", "sub"), None, None),
        ),
        out_specs=(P(None, "grp", "sub", None), P(None, "grp", "sub", None)),
        check_vma=False,
    )
```

```python
import jax
import jax.numpy as jnp
from jax import lax
from jax.experimental import pallas as pl
from jax.experimental.pallas import tpu as pltpu
from jax.sharding import PartitionSpec as P

BF = jnp.bfloat16
F32 = jnp.float32
MESH = pl.DeviceIdType.MESH
SWEEPS = 4


def split(x):
    hi = x.astype(BF)
    lo = (x - hi.astype(F32)).astype(BF)
    return hi, lo


def place(device):
    return (device // 16, device % 16)


def iota(shape, dim):
    return lax.broadcasted_iota(jnp.int32, shape, dim)


def build_table(field, table):
    for c in range(3):
        here = field[c].reshape(128, 256)
        for zc, x in enumerate((here, pltpu.roll(here, 255, 1))):
            hi, lo = split(x)
            for xx in range(8):
                at = xx * 96 + zc * 48 + c * 16
                table[at : at + 16, :] = hi[xx * 16 : xx * 16 + 16]
                table[768 + at : 784 + at, :] = lo[xx * 16 : xx * 16 + 16]


def interpolate_tile(t, cells, weights, out, table):
    z_iota = iota((256, 128), 0).astype(F32).astype(BF)
    y_iota = iota((16, 128), 0)
    tile = cells[0, pl.ds(pl.multiple_of(t * 8, 8), 8), :]
    z_tile = (tile & 255).astype(F32).astype(BF)
    y_tile = (tile >> 8) & 15
    x_tile = tile >> 12
    for pair in range(4):
        hot = [
            jnp.where(z_iota == z_tile[s : s + 1, :], jnp.ones((), BF), jnp.zeros((), BF))
            for s in (2 * pair, 2 * pair + 1)
        ]
        hot = jnp.concatenate(hot, axis=1)
        got = jnp.dot(table[0:768, :], hot, preferred_element_type=F32)
        got = got + jnp.dot(table[768:1536, :], hot, preferred_element_type=F32)
        for half in range(2):
            s = 2 * pair + half
            r = t * 8 + s
            w = weights[0, r]
            y_row = y_tile[s : s + 1, :]
            x_row = jnp.broadcast_to(x_tile[s : s + 1, :], (16, 128))
            y_here = y_iota == y_row
            y_next = y_iota == y_row + 1
            by_y = {}
            for a in range(2):
                for zc in range(2):
                    k = 4 * a + zc
                    by_y[a, zc] = jnp.where(
                        y_here, w[k : k + 1, :], jnp.where(y_next, w[k + 2 : k + 3, :], 0.0)
                    )
            acc = [None] * 3
            before = None
            for xx in range(8):
                here = x_row == xx if xx < 7 else None
                for zc in range(2):
                    coef = None
                    if before is not None:
                        coef = jnp.where(before, by_y[1, zc], 0.0)
                    if here is not None:
                        coef = jnp.where(here, by_y[0, zc], 0.0 if coef is None else coef)
                    for c in range(3):
                        at = xx * 96 + zc * 48 + c * 16
                        term = coef * got[at : at + 16, half * 128 : half * 128 + 128]
                        acc[c] = term if acc[c] is None else acc[c] + term
                before = here
            for c in range(3):
                out[r, c, :] = jnp.sum(acc[c], axis=0)


def interpolate(field, cells, weights, sent, table, beside):
    build_table(field, table)

    def step(i, carry):
        beside(i)
        interpolate_tile(i, cells, weights, sent, table)
        return carry

    lax.fori_loop(0, 16, step, 0)


def sender(sent, came, sems, me):
    def send(offset):
        target = (me + offset) % 128
        pltpu.make_async_remote_copy(
            src_ref=sent.at[target],
            dst_ref=came.at[me],
            send_sem=sems.at[0],
            recv_sem=sems.at[1],
            device_id=place(target),
            device_id_type=MESH,
        ).start()

    def first():
        for offset in range(1, 16):
            send(offset)
        came[me] = sent[me]

    def some(i):
        for n in range(7):
            send(16 + 7 * i + n)

    return first, some


def all_of(sent, came, sems, me):
    return pltpu.make_async_remote_copy(
        src_ref=sent.at[pl.ds(0, 127)],
        dst_ref=came.at[pl.ds(0, 127)],
        send_sem=sems.at[0],
        recv_sem=sems.at[1],
        device_id=place((me + 1) % 128),
        device_id_type=MESH,
    )


def overwrite(field, receptors, got, start, frozen, total, beside):
    z_iota = iota((256, 128), 0).astype(F32).astype(BF)
    r_iota = iota((128, 128), 0).astype(F32).astype(BF)
    lift = jnp.where(iota((4, 128), 0) == 0, 8.0, 0.0)
    one = jnp.ones((), BF)
    zero = jnp.zeros((), BF)
    total[...] = jnp.zeros_like(total)

    def step(i, carry):
        beside(i)
        tile = receptors[0, pl.ds(pl.multiple_of(i * 8, 8), 8), :]
        z_tile = (tile & 255).astype(F32).astype(BF)
        r_tile = (tile >> 8).astype(F32).astype(BF)
        for half in range(2):
            hots = []
            lefts = []
            for s in range(4 * half, 4 * half + 4):
                hots.append(jnp.where(z_iota == z_tile[s : s + 1, :], one, zero))
                mine = r_iota == r_tile[s : s + 1, :]
                parts = split(got[i * 8 + s] + lift)
                rows = [jnp.where(mine, p[c : c + 1, :], zero) for p in parts for c in range(3)]
                lefts.append(jnp.concatenate(rows, axis=0))
            total[...] += lax.dot_general(
                jnp.concatenate(lefts, axis=1),
                jnp.concatenate(hots, axis=1),
                (((1,), (1,)), ((), ())),
                preferred_element_type=F32,
            )
        return carry

    lax.fori_loop(0, 16, step, 0)
    mask = total[0:128, :]
    frozen[...] = mask.reshape(8, 16, 256)
    for c in range(3):
        value = total[c * 128 : c * 128 + 128, :] + total[384 + c * 128 : 512 + c * 128, :]
        if c == 0:
            value = value - 8.0
        old = field[c].reshape(128, 256)
        start[c, 1:9] = jnp.where(mask > 1.0, value, old).reshape(8, 16, 256)


def halo_copies(grid, k, velocity, edge, halo, send_sems, recv_sems, g, s):
    north, south = (s + 1) % 16, (s + 15) % 16
    plan = [
        (edge.at[grid, k, 0], halo.at[grid, k, 0], (g, north)),
        (edge.at[grid, k, 1], halo.at[grid, k, 1], (g, south)),
    ]
    if grid == 0:
        plan += [
            (velocity.at[k, :, 8], velocity.at[k, :, 0], ((g + 1) % 8, s)),
            (velocity.at[k, :, 1], velocity.at[k, :, 9], ((g + 7) % 8, s)),
        ]
    return [
        pltpu.make_async_remote_copy(
            src_ref=source,
            dst_ref=target,
            send_sem=send_sems.at[grid, k, n],
            recv_sem=recv_sems.at[grid, k, n],
            device_id=device,
            device_id_type=MESH,
        )
        for n, (source, target, device) in enumerate(plan)
    ]


def fill_edges(grid, k, velocity, edge):
    for c in range(3):
        edge[grid, k, 0, c] = velocity[k, c, 1:9, 15, :]
        edge[grid, k, 1, c] = velocity[k, c, 1:9, 0, :]


def shifted(plane, low, high):
    y = iota((16, 256), 0)
    after_y = jnp.where(y == 15, high, pltpu.roll(plane, 15, 0))
    before_y = jnp.where(y == 0, low, pltpu.roll(plane, 1, 0))
    return after_y, before_y, pltpu.roll(plane, 255, 1), pltpu.roll(plane, 1, 1)


def assemble(grid, velocity, halo, source, inertia, frozen, coef, rhs, rim, g, s):
    y = iota((16, 256), 0)
    z = iota((16, 256), 1)
    y_low = jnp.where(s > 0, 1.0, 0.0)
    y_high = jnp.where(s < 15, 1.0, 0.0)

    def face(middle, other, sign):
        return 1.0 + jnp.maximum(sign * (middle + other), 0.0)

    def step(x, carry):
        u, v, w = (velocity[0, c, x + 1] for c in range(3))
        if grid == 0:
            x_low = jnp.where((x > 0) | (g > 0), 1.0, 0.0)
            x_high = jnp.where((x < 7) | (g < 7), 1.0, 0.0)
        else:
            x_low = jnp.where(x > 0, 1.0, 0.0)
            x_high = jnp.where(x < 7, 1.0, 0.0)
        low = halo[grid, 0, 0, 1, pl.ds(x, 1), :] * y_low
        high = halo[grid, 0, 1, 1, pl.ds(x, 1), :] * y_high
        v_after, v_before, _, _ = shifted(v, low, high)
        w_after = jnp.where(z == 255, 0.0, pltpu.roll(w, 255, 1))
        w_before = jnp.where(z == 0, 0.0, pltpu.roll(w, 1, 1))
        faces = [
            face(u, velocity[0, 0, x + 2] * x_high, -0.5),
            face(u, velocity[0, 0, x] * x_low, 0.5),
            face(v, v_after, -0.5),
            face(v, v_before, 0.5),
            face(w, w_after, -0.5),
            face(w, w_before, 0.5),
        ]
        weight = inertia[x]
        diagonal = weight
        for f in faces:
            diagonal = diagonal + f
        inverse = 1.0 / diagonal
        stuck = frozen[x] > 1.0
        live = jnp.where(stuck, 0.0, inverse)
        faces = [f * live for f in faces]
        coef[0, x] = faces[0] * x_high
        coef[1, x] = faces[1] * x_low
        coef[2, x] = faces[2]
        coef[3, x] = faces[3]
        coef[4, x] = jnp.where(z == 255, 0.0, faces[4])
        coef[5, x] = jnp.where(z == 0, 0.0, faces[5])
        for c, start in enumerate((u, v, w)):
            right = (source[c, x] + weight * start) * inverse
            rhs[c, x] = jnp.where(stuck, start, right)
        return carry

    lax.fori_loop(0, 8, step, 0)
    rim[grid, 0] = coef[3, :, 0, :] * y_low
    rim[grid, 1] = coef[2, :, 15, :] * y_high
    coef[3, :, 0, :] = jnp.zeros((8, 256), F32)
    coef[2, :, 15, :] = jnp.zeros((8, 256), F32)


def inner(now, coef, rhs, after):
    for x in range(8):
        for c in range(3):
            plane = now[c, x + 1]
            total = rhs[c, x]
            if x < 7:
                total = total + coef[0, x] * now[c, x + 2]
            if x > 0:
                total = total + coef[1, x] * now[c, x]
            total = total + coef[2, x] * pltpu.roll(plane, 15, 0)
            total = total + coef[3, x] * pltpu.roll(plane, 1, 0)
            total = total + coef[4, x] * pltpu.roll(plane, 255, 1)
            total = total + coef[5, x] * pltpu.roll(plane, 1, 1)
            after[c, x] = total


def outer(grid, k, now, halo, coef, rim, after, edge):
    for c in range(3):
        if grid == 0:
            after[c, 0] = after[c, 0] + coef[1, 0] * now[c, 0]
            after[c, 7] = after[c, 7] + coef[0, 7] * now[c, 9]
        low = after[c, :, 0, :] + rim[grid, 0] * halo[grid, k, 0, c]
        high = after[c, :, 15, :] + rim[grid, 1] * halo[grid, k, 1, c]
        after[c, :, 0, :] = low
        after[c, :, 15, :] = high
        if k < SWEEPS - 1:
            edge[grid, k + 1, 0, c] = high
            edge[grid, k + 1, 1, c] = low


def kernel(*refs):
    (
        bg_vel_hbm, nb_vel_hbm, bg_source_hbm, nb_source_hbm, bg_inertia_hbm, nb_inertia_hbm,
        bg_cells_hbm, bg_weights_hbm, nb_cells_hbm, nb_weights_hbm, nb_rec_hbm, bg_rec_hbm,
        bg_out, nb_out,
        bg_vel, nb_vel, bg_source, nb_source, bg_inertia, nb_inertia,
        bg_cells, bg_weights, nb_cells, nb_weights, nb_rec, bg_rec,
        table, total,
        bg_sent, nb_sent, to_near, to_back, bg_run, nb_run,
        bg_frozen, nb_frozen, bg_coef, nb_coef, bg_rhs, nb_rhs, edge, halo, rim,
        load_sems, near_sems, back_sems, send_sems, recv_sems,
    ) = refs
    g = lax.axis_index("grp")
    s = lax.axis_index("sub")
    me = g * 16 + s

    hbm = refs[:12]
    vmem = refs[14:26]
    loads = [
        pltpu.make_async_copy(hbm[n], vmem[n], load_sems.at[n]) for n in range(12)
    ]
    for n in (0, 6, 7, 1, 8, 9, 10, 11, 2, 3, 4, 5):
        loads[n].start()

    barrier = pltpu.get_barrier_semaphore()

    def greet(i, carry):
        pl.semaphore_signal(
            barrier, inc=1, device_id=place((me + i) % 128), device_id_type=MESH
        )
        return carry

    lax.fori_loop(1, 128, greet, 0)
    for c in range(3):
        nb_run[0, c, 0] = jnp.zeros((16, 256), F32)
        nb_run[0, c, 9] = jnp.zeros((16, 256), F32)

    near_first, near_some = sender(bg_sent, to_near, near_sems, me)
    back_first, back_some = sender(nb_sent, to_back, back_sems, me)
    for n in (0, 6, 7):
        loads[n].wait()
    interpolate(bg_vel, bg_cells, bg_weights, bg_sent, table, lambda i: None)
    for n in (1, 8, 9):
        loads[n].wait()
    pl.semaphore_wait(barrier, 127)
    near_first()
    interpolate(nb_vel, nb_cells, nb_weights, nb_sent, table, near_some)
    for n in (10, 11, 2, 3, 4, 5):
        loads[n].wait()
    back_first()
    near = all_of(bg_sent, to_near, near_sems, me)
    near.wait_recv()
    overwrite(nb_vel, nb_rec, to_near, nb_run.at[0], nb_frozen, total, back_some)

    copies = []

    def exchange(grid, k, velocity):
        new = halo_copies(grid, k, velocity, edge, halo, send_sems, recv_sems, g, s)
        for copy in new:
            copy.start()
        copies.extend(new)
        return new

    fill_edges(1, 0, nb_run, edge)
    nb_moving = exchange(1, 0, nb_run)
    back = all_of(nb_sent, to_back, back_sems, me)
    back.wait_recv()
    overwrite(bg_vel, bg_rec, to_back, bg_run.at[0], bg_frozen, total, lambda i: None)
    fill_edges(0, 0, bg_run, edge)
    moving = [exchange(0, 0, bg_run), nb_moving]

    runs = (bg_run, nb_run)
    outs = (bg_out, nb_out)
    coefs = (bg_coef, nb_coef)
    sides = (bg_rhs, nb_rhs)
    fields = ((bg_source, bg_inertia, bg_frozen), (nb_source, nb_inertia, nb_frozen))
    for k in range(SWEEPS):
        for grid in (1, 0):
            run, coef, rhs = runs[grid], coefs[grid], sides[grid]
            now = run.at[k]
            after = run.at[k + 1, :, pl.ds(1, 8)] if k < SWEEPS - 1 else outs[grid]
            if k == 0:
                for copy in moving[grid]:
                    copy.wait_recv()
                assemble(grid, run, halo, *fields[grid], coef, rhs, rim, g, s)
            inner(now, coef, rhs, after)
            if k > 0:
                for copy in moving[grid]:
                    copy.wait_recv()
            outer(grid, k, now, halo, coef, rim, after, edge)
            if k < SWEEPS - 1:
                moving[grid] = exchange(grid, k + 1, run)

    near.wait_send()
    back.wait_send()
    for copy in copies:
        copy.wait_send()


def body(*args):
    out = jax.ShapeDtypeStruct((3, 8, 16, 256), F32)
    vmem = pltpu.VMEM
    return pl.pallas_call(
        kernel,
        out_shape=(out, out),
        in_specs=[pl.BlockSpec(memory_space=pl.ANY)] * 12,
        out_specs=[pl.BlockSpec(memory_space=vmem)] * 2,
        scratch_shapes=[vmem(a.shape, a.dtype) for a in args]
        + [
            vmem((1536, 256), BF),
            vmem((768, 256), F32),
            vmem((128, 4, 128), F32),
            vmem((128, 4, 128), F32),
            vmem((128, 4, 128), F32),
            vmem((128, 4, 128), F32),
            vmem((SWEEPS, 3, 10, 16, 256), F32),
            vmem((SWEEPS, 3, 10, 16, 256), F32),
            vmem((8, 16, 256), F32),
            vmem((8, 16, 256), F32),
            vmem((6, 8, 16, 256), F32),
            vmem((6, 8, 16, 256), F32),
            vmem((3, 8, 16, 256), F32),
            vmem((3, 8, 16, 256), F32),
            vmem((2, SWEEPS, 2, 3, 8, 256), F32),
            vmem((2, SWEEPS, 2, 3, 8, 256), F32),
            vmem((2, 2, 8, 256), F32),
            pltpu.SemaphoreType.DMA((12,)),
            pltpu.SemaphoreType.DMA((2,)),
            pltpu.SemaphoreType.DMA((2,)),
            pltpu.SemaphoreType.DMA((2, SWEEPS, 4)),
            pltpu.SemaphoreType.DMA((2, SWEEPS, 4)),
        ],
        compiler_params=pltpu.CompilerParams(
            collective_id=0, has_side_effects=True, vmem_limit_bytes=63 * 2**20
        ),
        name="overset",
    )(*args)


def solution(mesh):
    return jax.shard_map(
        body,
        mesh=mesh,
        in_specs=(
            P(None, "grp", "sub", None),
            P(None, "grp", "sub", None),
            P(None, "grp", "sub", None),
            P(None, "grp", "sub", None),
            P("grp", "sub", None),
            P("grp", "sub", None),
            P(("grp", "sub"), None, None),
            P(("grp", "sub"), None, None, None),
            P(("grp", "sub"), None, None),
            P(("grp", "sub"), None, None, None),
            P(("grp", "sub"), None, None),
            P(("grp", "sub"), None, None),
        ),
        out_specs=(P(None, "grp", "sub", None), P(None, "grp", "sub", None)),
        check_vma=False,
    )
```

```python
import jax
import jax.numpy as jnp
from jax import lax
from jax.experimental import pallas as pl
from jax.experimental.pallas import tpu as pltpu
from jax.sharding import PartitionSpec as P

BF = jnp.bfloat16
F32 = jnp.float32
MESH = pl.DeviceIdType.MESH
SWEEPS = 4
HOP_STEP = 7


def split(x):
    hi = x.astype(BF)
    lo = (x - hi.astype(F32)).astype(BF)
    return hi, lo


def iota(shape, dim):
    return lax.broadcasted_iota(jnp.int32, shape, dim)


def build_table(field, table):
    for c in range(3):
        here = field[c].reshape(128, 256)
        for zc, x in enumerate((here, pltpu.roll(here, 255, 1))):
            hi, lo = split(x)
            for xx in range(8):
                at = xx * 96 + zc * 48 + c * 16
                table[at : at + 16, :] = hi[xx * 16 : xx * 16 + 16]
                table[768 + at : 784 + at, :] = lo[xx * 16 : xx * 16 + 16]


def interpolate_tile(t, cells, weights, out, table):
    z_iota = iota((256, 128), 0).astype(F32).astype(BF)
    y_iota = iota((16, 128), 0)
    tile = cells[0, pl.ds(pl.multiple_of(t * 8, 8), 8), :]
    z_tile = (tile & 255).astype(F32).astype(BF)
    y_tile = (tile >> 8) & 15
    x_tile = tile >> 12
    for pair in range(4):
        hot = [
            jnp.where(z_iota == z_tile[s : s + 1, :], jnp.ones((), BF), jnp.zeros((), BF))
            for s in (2 * pair, 2 * pair + 1)
        ]
        hot = jnp.concatenate(hot, axis=1)
        got = jnp.dot(table[0:768, :], hot, preferred_element_type=F32)
        got = got + jnp.dot(table[768:1536, :], hot, preferred_element_type=F32)
        for half in range(2):
            s = 2 * pair + half
            w = weights[0, t * 8 + s]
            y_row = y_tile[s : s + 1, :]
            x_row = jnp.broadcast_to(x_tile[s : s + 1, :], (16, 128))
            y_here = y_iota == y_row
            y_next = y_iota == y_row + 1
            by_y = {}
            for a in range(2):
                for zc in range(2):
                    k = 4 * a + zc
                    by_y[a, zc] = jnp.where(
                        y_here, w[k : k + 1, :], jnp.where(y_next, w[k + 2 : k + 3, :], 0.0)
                    )
            acc = [None] * 3
            before = None
            for xx in range(8):
                here = x_row == xx if xx < 7 else None
                for zc in range(2):
                    coef = None
                    if before is not None:
                        coef = jnp.where(before, by_y[1, zc], 0.0)
                    if here is not None:
                        coef = jnp.where(here, by_y[0, zc], 0.0 if coef is None else coef)
                    for c in range(3):
                        at = xx * 96 + zc * 48 + c * 16
                        term = coef * got[at : at + 16, half * 128 : half * 128 + 128]
                        acc[c] = term if acc[c] is None else acc[c] + term
                before = here
            for c in range(3):
                out[t // 2, (t % 2) * 8 + s, c, :] = jnp.sum(acc[c], axis=0)


def interpolate(field, cells, weights, sent, table, beside):
    build_table(field, table)

    def step(i, carry):
        beside(i)
        interpolate_tile(i, cells, weights, sent, table)
        return carry

    lax.fori_loop(0, 16, step, 0)


class Exchange:
    def __init__(self, sent, held, came, sems, g, s):
        self.sent, self.held, self.came, self.sems, self.g, self.s = sent, held, came, sems, g, s

    def across(self, offset):
        peer = (self.g + offset) % 8
        return pltpu.make_async_remote_copy(
            src_ref=self.sent.at[peer],
            dst_ref=self.held.at[self.g],
            send_sem=self.sems.at[0],
            recv_sem=self.sems.at[1],
            device_id=(peer, self.s),
            device_id_type=MESH,
        )

    def along(self, offset):
        peer = (self.s + offset) % 16
        return pltpu.make_async_remote_copy(
            src_ref=self.held.at[:, peer],
            dst_ref=self.came.at[self.s],
            send_sem=self.sems.at[2],
            recv_sem=self.sems.at[3],
            device_id=(self.g, peer),
            device_id_type=MESH,
        )

    def all_across(self):
        return pltpu.make_async_remote_copy(
            src_ref=self.sent.at[pl.ds(0, 7)],
            dst_ref=self.held.at[pl.ds(0, 7)],
            send_sem=self.sems.at[0],
            recv_sem=self.sems.at[1],
            device_id=((self.g + 1) % 8, self.s),
            device_id_type=MESH,
        )

    def all_along(self):
        return pltpu.make_async_remote_copy(
            src_ref=self.came.at[pl.ds(0, 15)],
            dst_ref=self.came.at[pl.ds(0, 15)],
            send_sem=self.sems.at[2],
            recv_sem=self.sems.at[3],
            device_id=(self.g, (self.s + 1) % 16),
            device_id_type=MESH,
        )

    def first_hop(self):
        for offset in (4, 3, 5, 2, 6, 1, 7):
            self.across(offset).start()
        self.held[self.g] = self.sent[self.g]

    def second_hop(self, i):
        @pl.when(i == HOP_STEP)
        def _():
            self.all_across().wait_recv()
            for offset in range(1, 16):
                self.along(offset).start()
            self.came[self.s] = self.held[:, self.s]

    def arrive(self):
        self.all_along().wait_recv()

    def finish(self):
        self.all_across().wait_send()
        self.all_along().wait_send()


def overwrite(field, receptors, got, start, frozen, total, beside):
    z_iota = iota((256, 128), 0).astype(F32).astype(BF)
    r_iota = iota((128, 128), 0).astype(F32).astype(BF)
    lift = jnp.where(iota((4, 128), 0) == 0, 8.0, 0.0)
    one = jnp.ones((), BF)
    zero = jnp.zeros((), BF)
    total[...] = jnp.zeros_like(total)

    def step(i, carry):
        beside(i)
        tile = receptors[0, pl.ds(pl.multiple_of(i * 8, 8), 8), :]
        z_tile = (tile & 255).astype(F32).astype(BF)
        r_tile = (tile >> 8).astype(F32).astype(BF)
        for half in range(2):
            hots = []
            lefts = []
            for s in range(4 * half, 4 * half + 4):
                hots.append(jnp.where(z_iota == z_tile[s : s + 1, :], one, zero))
                mine = r_iota == r_tile[s : s + 1, :]
                parts = split(got[(i % 2) * 8 + s, i // 2] + lift)
                rows = [jnp.where(mine, p[c : c + 1, :], zero) for p in parts for c in range(3)]
                lefts.append(jnp.concatenate(rows, axis=0))
            total[...] += lax.dot_general(
                jnp.concatenate(lefts, axis=1),
                jnp.concatenate(hots, axis=1),
                (((1,), (1,)), ((), ())),
                preferred_element_type=F32,
            )
        return carry

    lax.fori_loop(0, 16, step, 0)
    mask = total[0:128, :]
    frozen[...] = mask.reshape(8, 16, 256)
    for c in range(3):
        value = total[c * 128 : c * 128 + 128, :] + total[384 + c * 128 : 512 + c * 128, :]
        if c == 0:
            value = value - 8.0
        old = field[c].reshape(128, 256)
        start[c, 1:9] = jnp.where(mask > 1.0, value, old).reshape(8, 16, 256)


def halo_copies(grid, k, velocity, edge, halo, send_sems, recv_sems, g, s):
    north, south = (s + 1) % 16, (s + 15) % 16
    plan = [
        (edge.at[grid, k, 0], halo.at[grid, k, 0], (g, north)),
        (edge.at[grid, k, 1], halo.at[grid, k, 1], (g, south)),
    ]
    if grid == 0:
        plan += [
            (velocity.at[k, :, 8], velocity.at[k, :, 0], ((g + 1) % 8, s)),
            (velocity.at[k, :, 1], velocity.at[k, :, 9], ((g + 7) % 8, s)),
        ]
    return [
        pltpu.make_async_remote_copy(
            src_ref=source,
            dst_ref=target,
            send_sem=send_sems.at[grid, k, n],
            recv_sem=recv_sems.at[grid, k, n],
            device_id=device,
            device_id_type=MESH,
        )
        for n, (source, target, device) in enumerate(plan)
    ]


def fill_edges(grid, k, velocity, edge):
    for c in range(3):
        edge[grid, k, 0, c] = velocity[k, c, 1:9, 15, :]
        edge[grid, k, 1, c] = velocity[k, c, 1:9, 0, :]


def shifted(plane, low, high):
    y = iota((16, 256), 0)
    after_y = jnp.where(y == 15, high, pltpu.roll(plane, 15, 0))
    before_y = jnp.where(y == 0, low, pltpu.roll(plane, 1, 0))
    return after_y, before_y, pltpu.roll(plane, 255, 1), pltpu.roll(plane, 1, 1)


def assemble(grid, velocity, halo, source, inertia, frozen, coef, rhs, rim, g, s):
    y = iota((16, 256), 0)
    z = iota((16, 256), 1)
    y_low = jnp.where(s > 0, 1.0, 0.0)
    y_high = jnp.where(s < 15, 1.0, 0.0)

    def face(middle, other, sign):
        return 1.0 + jnp.maximum(sign * (middle + other), 0.0)

    def step(x, carry):
        u, v, w = (velocity[0, c, x + 1] for c in range(3))
        if grid == 0:
            x_low = jnp.where((x > 0) | (g > 0), 1.0, 0.0)
            x_high = jnp.where((x < 7) | (g < 7), 1.0, 0.0)
        else:
            x_low = jnp.where(x > 0, 1.0, 0.0)
            x_high = jnp.where(x < 7, 1.0, 0.0)
        low = halo[grid, 0, 0, 1, pl.ds(x, 1), :] * y_low
        high = halo[grid, 0, 1, 1, pl.ds(x, 1), :] * y_high
        v_after, v_before, _, _ = shifted(v, low, high)
        w_after = jnp.where(z == 255, 0.0, pltpu.roll(w, 255, 1))
        w_before = jnp.where(z == 0, 0.0, pltpu.roll(w, 1, 1))
        faces = [
            face(u, velocity[0, 0, x + 2] * x_high, -0.5),
            face(u, velocity[0, 0, x] * x_low, 0.5),
            face(v, v_after, -0.5),
            face(v, v_before, 0.5),
            face(w, w_after, -0.5),
            face(w, w_before, 0.5),
        ]
        weight = inertia[x]
        diagonal = weight
        for f in faces:
            diagonal = diagonal + f
        inverse = 1.0 / diagonal
        stuck = frozen[x] > 1.0
        live = jnp.where(stuck, 0.0, inverse)
        faces = [f * live for f in faces]
        coef[0, x] = faces[0] * x_high
        coef[1, x] = faces[1] * x_low
        coef[2, x] = faces[2]
        coef[3, x] = faces[3]
        coef[4, x] = jnp.where(z == 255, 0.0, faces[4])
        coef[5, x] = jnp.where(z == 0, 0.0, faces[5])
        for c, start in enumerate((u, v, w)):
            right = (source[c, x] + weight * start) * inverse
            rhs[c, x] = jnp.where(stuck, start, right)
        return carry

    lax.fori_loop(0, 8, step, 0)
    rim[grid, 0] = coef[3, :, 0, :] * y_low
    rim[grid, 1] = coef[2, :, 15, :] * y_high
    coef[3, :, 0, :] = jnp.zeros((8, 256), F32)
    coef[2, :, 15, :] = jnp.zeros((8, 256), F32)


def inner(now, coef, rhs, after):
    for x in range(8):
        for c in range(3):
            plane = now[c, x + 1]
            total = rhs[c, x]
            if x < 7:
                total = total + coef[0, x] * now[c, x + 2]
            if x > 0:
                total = total + coef[1, x] * now[c, x]
            total = total + coef[2, x] * pltpu.roll(plane, 15, 0)
            total = total + coef[3, x] * pltpu.roll(plane, 1, 0)
            total = total + coef[4, x] * pltpu.roll(plane, 255, 1)
            total = total + coef[5, x] * pltpu.roll(plane, 1, 1)
            after[c, x] = total


def outer(grid, k, now, halo, coef, rim, after, edge):
    for c in range(3):
        if grid == 0:
            after[c, 0] = after[c, 0] + coef[1, 0] * now[c, 0]
            after[c, 7] = after[c, 7] + coef[0, 7] * now[c, 9]
        low = after[c, :, 0, :] + rim[grid, 0] * halo[grid, k, 0, c]
        high = after[c, :, 15, :] + rim[grid, 1] * halo[grid, k, 1, c]
        after[c, :, 0, :] = low
        after[c, :, 15, :] = high
        if k < SWEEPS - 1:
            edge[grid, k + 1, 0, c] = high
            edge[grid, k + 1, 1, c] = low


def kernel(*refs):
    (
        bg_vel_hbm, nb_vel_hbm, bg_source_hbm, nb_source_hbm, bg_inertia_hbm, nb_inertia_hbm,
        bg_cells_hbm, bg_weights_hbm, nb_cells_hbm, nb_weights_hbm, nb_rec_hbm, bg_rec_hbm,
        bg_out, nb_out,
        bg_vel, nb_vel, bg_source, nb_source, bg_inertia, nb_inertia,
        bg_cells, bg_weights, nb_cells, nb_weights, nb_rec, bg_rec,
        table, total,
        bg_sent, nb_sent, bg_held, nb_held, to_near, to_back, bg_run, nb_run,
        bg_frozen, nb_frozen, bg_coef, nb_coef, bg_rhs, nb_rhs, edge, halo, rim,
        load_sems, near_sems, back_sems, send_sems, recv_sems,
    ) = refs
    g = lax.axis_index("grp")
    s = lax.axis_index("sub")

    hbm = refs[:12]
    vmem = refs[14:26]
    loads = [
        pltpu.make_async_copy(hbm[n], vmem[n], load_sems.at[n]) for n in range(12)
    ]
    for n in (0, 6, 7, 1, 8, 9, 10, 11, 2, 3, 4, 5):
        loads[n].start()

    barrier = pltpu.get_barrier_semaphore()

    for offset in range(1, 8):
        pl.semaphore_signal(
            barrier, inc=1, device_id=((g + offset) % 8, s), device_id_type=MESH
        )
    for offset in range(1, 16):
        pl.semaphore_signal(
            barrier, inc=1, device_id=(g, (s + offset) % 16), device_id_type=MESH
        )
    for c in range(3):
        nb_run[0, c, 0] = jnp.zeros((16, 256), F32)
        nb_run[0, c, 9] = jnp.zeros((16, 256), F32)

    near = Exchange(bg_sent, bg_held, to_near, near_sems, g, s)
    back = Exchange(nb_sent, nb_held, to_back, back_sems, g, s)
    for n in (0, 6, 7):
        loads[n].wait()
    interpolate(bg_vel, bg_cells, bg_weights, bg_sent, table, lambda i: None)
    for n in (1, 8, 9):
        loads[n].wait()
    pl.semaphore_wait(barrier, 22)
    near.first_hop()
    interpolate(nb_vel, nb_cells, nb_weights, nb_sent, table, near.second_hop)
    for n in (10, 11, 2, 3, 4, 5):
        loads[n].wait()
    back.first_hop()
    near.arrive()
    overwrite(nb_vel, nb_rec, to_near, nb_run.at[0], nb_frozen, total, back.second_hop)

    copies = []

    def exchange(grid, k, velocity):
        new = halo_copies(grid, k, velocity, edge, halo, send_sems, recv_sems, g, s)
        for copy in new:
            copy.start()
        copies.extend(new)
        return new

    fill_edges(1, 0, nb_run, edge)
    nb_moving = exchange(1, 0, nb_run)
    back.arrive()
    overwrite(bg_vel, bg_rec, to_back, bg_run.at[0], bg_frozen, total, lambda i: None)
    fill_edges(0, 0, bg_run, edge)
    moving = [exchange(0, 0, bg_run), nb_moving]

    runs = (bg_run, nb_run)
    outs = (bg_out, nb_out)
    coefs = (bg_coef, nb_coef)
    sides = (bg_rhs, nb_rhs)
    fields = ((bg_source, bg_inertia, bg_frozen), (nb_source, nb_inertia, nb_frozen))
    for k in range(SWEEPS):
        for grid in (1, 0):
            run, coef, rhs = runs[grid], coefs[grid], sides[grid]
            now = run.at[k]
            after = run.at[k + 1, :, pl.ds(1, 8)] if k < SWEEPS - 1 else outs[grid]
            if k == 0:
                for copy in moving[grid]:
                    copy.wait_recv()
                assemble(grid, run, halo, *fields[grid], coef, rhs, rim, g, s)
            inner(now, coef, rhs, after)
            if k > 0:
                for copy in moving[grid]:
                    copy.wait_recv()
            outer(grid, k, now, halo, coef, rim, after, edge)
            if k < SWEEPS - 1:
                moving[grid] = exchange(grid, k + 1, run)

    near.finish()
    back.finish()
    for copy in copies:
        copy.wait_send()


def body(*args):
    out = jax.ShapeDtypeStruct((3, 8, 16, 256), F32)
    vmem = pltpu.VMEM
    return pl.pallas_call(
        kernel,
        out_shape=(out, out),
        in_specs=[pl.BlockSpec(memory_space=pl.ANY)] * 12,
        out_specs=[pl.BlockSpec(memory_space=vmem)] * 2,
        scratch_shapes=[vmem(a.shape, a.dtype) for a in args]
        + [
            vmem((1536, 256), BF),
            vmem((768, 256), F32),
            vmem((8, 16, 4, 128), F32),
            vmem((8, 16, 4, 128), F32),
            vmem((8, 16, 4, 128), F32),
            vmem((8, 16, 4, 128), F32),
            vmem((16, 8, 4, 128), F32),
            vmem((16, 8, 4, 128), F32),
            vmem((SWEEPS, 3, 10, 16, 256), F32),
            vmem((SWEEPS, 3, 10, 16, 256), F32),
            vmem((8, 16, 256), F32),
            vmem((8, 16, 256), F32),
            vmem((6, 8, 16, 256), F32),
            vmem((6, 8, 16, 256), F32),
            vmem((3, 8, 16, 256), F32),
            vmem((3, 8, 16, 256), F32),
            vmem((2, SWEEPS, 2, 3, 8, 256), F32),
            vmem((2, SWEEPS, 2, 3, 8, 256), F32),
            vmem((2, 2, 8, 256), F32),
            pltpu.SemaphoreType.DMA((12,)),
            pltpu.SemaphoreType.DMA((4,)),
            pltpu.SemaphoreType.DMA((4,)),
            pltpu.SemaphoreType.DMA((2, SWEEPS, 4)),
            pltpu.SemaphoreType.DMA((2, SWEEPS, 4)),
        ],
        compiler_params=pltpu.CompilerParams(
            collective_id=0, has_side_effects=True, vmem_limit_bytes=63 * 2**20
        ),
        name="overset",
    )(*args)


def solution(mesh):
    return jax.shard_map(
        body,
        mesh=mesh,
        in_specs=(
            P(None, "grp", "sub", None),
            P(None, "grp", "sub", None),
            P(None, "grp", "sub", None),
            P(None, "grp", "sub", None),
            P("grp", "sub", None),
            P("grp", "sub", None),
            P(("grp", "sub"), None, None),
            P(("grp", "sub"), None, None, None),
            P(("grp", "sub"), None, None),
            P(("grp", "sub"), None, None, None),
            P(("grp", "sub"), None, None),
            P(("grp", "sub"), None, None),
        ),
        out_specs=(P(None, "grp", "sub", None), P(None, "grp", "sub", None)),
        check_vma=False,
    )
```

```python
import jax
import jax.numpy as jnp
from jax import lax
from jax.experimental import pallas as pl
from jax.experimental.pallas import tpu as pltpu
from jax.sharding import PartitionSpec as P

BF = jnp.bfloat16
F32 = jnp.float32
F8 = jnp.float8_e4m3fn
LOW = 256.0
TINY = 1e-30
MESH = pl.DeviceIdType.MESH
SWEEPS = 4
HOP_STEP = 7


def split(x):
    hi = x.astype(BF)
    lo = ((x - hi.astype(F32)) * LOW).astype(BF)
    return hi, lo


def iota(shape, dim):
    return lax.broadcasted_iota(jnp.int32, shape, dim)


def scales(peak):
    peak = jnp.maximum(jnp.max(jnp.max(peak, axis=0, keepdims=True), axis=1, keepdims=True), 1e-30)
    return 4.0 / peak, peak * 0.25


def build_table(field, high, low, low8):
    peak = jnp.maximum(jnp.maximum(jnp.abs(field[0]), jnp.abs(field[1])), jnp.abs(field[2]))
    scale, back = scales(peak.reshape(128, 256))
    for c in range(3):
        here = field[c].reshape(128, 256) * scale
        for zc, x in enumerate((here, pltpu.roll(here, 255, 1))):
            hi, lo = split(x)
            for xx in range(8):
                at = xx * 96 + zc * 48 + c * 16
                high[at : at + 16, :] = hi[xx * 16 : xx * 16 + 16]
                low[at : at + 16, :] = lo[xx * 16 : xx * 16 + 16]
    low8[...] = low[...].astype(F8)
    return back


def interpolate_tile(t, cells, weights, out, high, low8, back):
    z_iota = iota((256, 128), 0).astype(F32).astype(BF)
    y_iota = iota((16, 128), 0)
    tile = cells[0, pl.ds(pl.multiple_of(t * 8, 8), 8), :]
    z_tile = (tile & 255).astype(F32).astype(BF)
    y_tile = (tile >> 8) & 15
    x_tile = tile >> 12
    for pair in range(4):
        hot = [
            jnp.where(z_iota == z_tile[s : s + 1, :], jnp.ones((), BF), jnp.zeros((), BF))
            for s in (2 * pair, 2 * pair + 1)
        ]
        hot = jnp.concatenate(hot, axis=1)
        hot8 = (hot * (1.0 / LOW)).astype(F8)
        got = jnp.dot(high[...], hot, preferred_element_type=F32)
        got = got + jnp.dot(low8[...], hot8, preferred_element_type=F32)
        for half in range(2):
            s = 2 * pair + half
            w = weights[0, t * 8 + s]
            y_row = y_tile[s : s + 1, :]
            x_row = jnp.broadcast_to(x_tile[s : s + 1, :], (16, 128))
            y_here = y_iota == y_row
            y_next = y_iota == y_row + 1
            by_y = {}
            for a in range(2):
                for zc in range(2):
                    k = 4 * a + zc
                    by_y[a, zc] = jnp.where(
                        y_here, w[k : k + 1, :], jnp.where(y_next, w[k + 2 : k + 3, :], 0.0)
                    )
            acc = [None] * 3
            before = None
            for xx in range(8):
                here = x_row == xx if xx < 7 else None
                for zc in range(2):
                    coef = None
                    if before is not None:
                        coef = jnp.where(before, by_y[1, zc], 0.0)
                    if here is not None:
                        coef = jnp.where(here, by_y[0, zc], 0.0 if coef is None else coef)
                    for c in range(3):
                        at = xx * 96 + zc * 48 + c * 16
                        term = coef * got[at : at + 16, half * 128 : half * 128 + 128]
                        acc[c] = term if acc[c] is None else acc[c] + term
                before = here
            for c in range(3):
                out[t // 2, (t % 2) * 8 + s, c, :] = jnp.sum(acc[c], axis=0) * back[0]


def interpolate(field, cells, weights, sent, tables, beside):
    high, low, low8 = tables
    back = build_table(field, high, low, low8)

    def step(i, carry):
        beside(i)
        interpolate_tile(i, cells, weights, sent, high, low8, back)
        return carry

    lax.fori_loop(0, 16, step, 0)


class Exchange:
    def __init__(self, sent, held, came, sems, g, s):
        self.sent, self.held, self.came, self.sems, self.g, self.s = sent, held, came, sems, g, s

    def across(self, offset):
        peer = (self.g + offset) % 8
        return pltpu.make_async_remote_copy(
            src_ref=self.sent.at[peer],
            dst_ref=self.held.at[self.g],
            send_sem=self.sems.at[0],
            recv_sem=self.sems.at[1],
            device_id=(peer, self.s),
            device_id_type=MESH,
        )

    def along(self, offset):
        peer = (self.s + offset) % 16
        return pltpu.make_async_remote_copy(
            src_ref=self.held.at[:, peer],
            dst_ref=self.came.at[self.s],
            send_sem=self.sems.at[2],
            recv_sem=self.sems.at[3],
            device_id=(self.g, peer),
            device_id_type=MESH,
        )

    def all_across(self):
        return pltpu.make_async_remote_copy(
            src_ref=self.sent.at[pl.ds(0, 7)],
            dst_ref=self.held.at[pl.ds(0, 7)],
            send_sem=self.sems.at[0],
            recv_sem=self.sems.at[1],
            device_id=((self.g + 1) % 8, self.s),
            device_id_type=MESH,
        )

    def all_along(self):
        return pltpu.make_async_remote_copy(
            src_ref=self.came.at[pl.ds(0, 15)],
            dst_ref=self.came.at[pl.ds(0, 15)],
            send_sem=self.sems.at[2],
            recv_sem=self.sems.at[3],
            device_id=(self.g, (self.s + 1) % 16),
            device_id_type=MESH,
        )

    def first_hop(self):
        for offset in (4, 3, 5, 2, 6, 1, 7):
            self.across(offset).start()
        self.held[self.g] = self.sent[self.g]

    def second_hop(self, i):
        @pl.when(i == HOP_STEP)
        def _():
            self.all_across().wait_recv()
            for offset in range(1, 16):
                self.along(offset).start()
            self.came[self.s] = self.held[:, self.s]

    def arrive(self):
        self.all_along().wait_recv()

    def finish(self):
        self.all_across().wait_send()
        self.all_along().wait_send()


def overwrite(field, receptors, got, start, frozen, total, beside):
    z_iota = iota((256, 128), 0).astype(F32).astype(BF)
    r_iota = iota((128, 128), 0).astype(F32).astype(BF)
    row = iota((4, 128), 0)
    peak = jnp.zeros((4, 128), F32)
    for p in range(16):
        peak = jnp.maximum(peak, jnp.max(jnp.abs(got[p]), axis=0))
    scale, back = scales(jnp.where(row < 3, peak, 0.0))
    one = jnp.ones((), BF)
    zero = jnp.zeros((), BF)
    total[...] = jnp.zeros_like(total)

    def step(i, carry):
        beside(i)
        tile = receptors[0, pl.ds(pl.multiple_of(i * 8, 8), 8), :]
        z_tile = (tile & 255).astype(F32).astype(BF)
        r_tile = (tile >> 8).astype(F32).astype(BF)
        for half in range(2):
            hots = []
            highs = []
            lows = []
            for s in range(4 * half, 4 * half + 4):
                hots.append(jnp.where(z_iota == z_tile[s : s + 1, :], one, zero))
                mine = r_iota == r_tile[s : s + 1, :]
                hi, lo = split(got[(i % 2) * 8 + s, i // 2] * scale)
                hi = hi.astype(F32)
                hi = jnp.where((hi == 0.0) & (row == 0), TINY, hi).astype(BF)
                for rows, part in ((highs, hi), (lows, lo)):
                    picked = [jnp.where(mine, part[c : c + 1, :], zero) for c in range(3)]
                    rows.append(jnp.concatenate(picked, axis=0))
            hot = jnp.concatenate(hots, axis=1)
            hot8 = (hot * (1.0 / LOW)).astype(F8)
            over_slots = (((1,), (1,)), ((), ()))
            total[...] += lax.dot_general(
                jnp.concatenate(highs, axis=1), hot, over_slots, preferred_element_type=F32
            ) + lax.dot_general(
                jnp.concatenate(lows, axis=1).astype(F8),
                hot8,
                over_slots,
                preferred_element_type=F32,
            )
        return carry

    lax.fori_loop(0, 16, step, 0)
    mask = total[0:128, :] != 0.0
    frozen[...] = jnp.where(mask, 1.0, 0.0).reshape(8, 16, 256)
    for c in range(3):
        value = total[c * 128 : c * 128 + 128, :]
        if c == 0:
            value = jnp.where(jnp.abs(value) < 2.0 * TINY, 0.0, value)
        old = field[c].reshape(128, 256)
        start[c, 1:9] = jnp.where(mask, value * back, old).reshape(8, 16, 256)


def halo_copies(grid, k, velocity, edge, halo, send_sems, recv_sems, g, s):
    north, south = (s + 1) % 16, (s + 15) % 16
    plan = [
        (edge.at[grid, k, 0], halo.at[grid, k, 0], (g, north)),
        (edge.at[grid, k, 1], halo.at[grid, k, 1], (g, south)),
    ]
    if grid == 0:
        plan += [
            (velocity.at[k, :, 8], velocity.at[k, :, 0], ((g + 1) % 8, s)),
            (velocity.at[k, :, 1], velocity.at[k, :, 9], ((g + 7) % 8, s)),
        ]
    return [
        pltpu.make_async_remote_copy(
            src_ref=source,
            dst_ref=target,
            send_sem=send_sems.at[grid, k, n],
            recv_sem=recv_sems.at[grid, k, n],
            device_id=device,
            device_id_type=MESH,
        )
        for n, (source, target, device) in enumerate(plan)
    ]


def fill_edges(grid, k, velocity, edge):
    for c in range(3):
        edge[grid, k, 0, c] = velocity[k, c, 1:9, 15, :]
        edge[grid, k, 1, c] = velocity[k, c, 1:9, 0, :]


def shifted(plane, low, high):
    y = iota((16, 256), 0)
    after_y = jnp.where(y == 15, high, pltpu.roll(plane, 15, 0))
    before_y = jnp.where(y == 0, low, pltpu.roll(plane, 1, 0))
    return after_y, before_y, pltpu.roll(plane, 255, 1), pltpu.roll(plane, 1, 1)


def assemble(grid, velocity, halo, source, inertia, frozen, coef, rhs, rim, g, s):
    y = iota((16, 256), 0)
    z = iota((16, 256), 1)
    y_low = jnp.where(s > 0, 1.0, 0.0)
    y_high = jnp.where(s < 15, 1.0, 0.0)

    def face(middle, other, sign):
        return 1.0 + jnp.maximum(sign * (middle + other), 0.0)

    def step(x, carry):
        u, v, w = (velocity[0, c, x + 1] for c in range(3))
        if grid == 0:
            x_low = jnp.where((x > 0) | (g > 0), 1.0, 0.0)
            x_high = jnp.where((x < 7) | (g < 7), 1.0, 0.0)
        else:
            x_low = jnp.where(x > 0, 1.0, 0.0)
            x_high = jnp.where(x < 7, 1.0, 0.0)
        low = halo[grid, 0, 0, 1, pl.ds(x, 1), :] * y_low
        high = halo[grid, 0, 1, 1, pl.ds(x, 1), :] * y_high
        v_after, v_before, _, _ = shifted(v, low, high)
        w_after = jnp.where(z == 255, 0.0, pltpu.roll(w, 255, 1))
        w_before = jnp.where(z == 0, 0.0, pltpu.roll(w, 1, 1))
        faces = [
            face(u, velocity[0, 0, x + 2] * x_high, -0.5),
            face(u, velocity[0, 0, x] * x_low, 0.5),
            face(v, v_after, -0.5),
            face(v, v_before, 0.5),
            face(w, w_after, -0.5),
            face(w, w_before, 0.5),
        ]
        weight = inertia[x]
        diagonal = weight
        for f in faces:
            diagonal = diagonal + f
        inverse = 1.0 / diagonal
        stuck = frozen[x] > 0.5
        live = jnp.where(stuck, 0.0, inverse)
        faces = [f * live for f in faces]
        coef[0, x] = faces[0] * x_high
        coef[1, x] = faces[1] * x_low
        coef[2, x] = faces[2]
        coef[3, x] = faces[3]
        coef[4, x] = jnp.where(z == 255, 0.0, faces[4])
        coef[5, x] = jnp.where(z == 0, 0.0, faces[5])
        for c, start in enumerate((u, v, w)):
            right = (source[c, x] + weight * start) * inverse
            rhs[c, x] = jnp.where(stuck, start, right)
        return carry

    lax.fori_loop(0, 8, step, 0)
    rim[grid, 0] = coef[3, :, 0, :] * y_low
    rim[grid, 1] = coef[2, :, 15, :] * y_high
    coef[3, :, 0, :] = jnp.zeros((8, 256), F32)
    coef[2, :, 15, :] = jnp.zeros((8, 256), F32)


def inner(now, coef, rhs, after):
    for x in range(8):
        for c in range(3):
            plane = now[c, x + 1]
            total = rhs[c, x]
            if x < 7:
                total = total + coef[0, x] * now[c, x + 2]
            if x > 0:
                total = total + coef[1, x] * now[c, x]
            total = total + coef[2, x] * pltpu.roll(plane, 15, 0)
            total = total + coef[3, x] * pltpu.roll(plane, 1, 0)
            total = total + coef[4, x] * pltpu.roll(plane, 255, 1)
            total = total + coef[5, x] * pltpu.roll(plane, 1, 1)
            after[c, x] = total


def outer(grid, k, now, halo, coef, rim, after, edge):
    for c in range(3):
        if grid == 0:
            after[c, 0] = after[c, 0] + coef[1, 0] * now[c, 0]
            after[c, 7] = after[c, 7] + coef[0, 7] * now[c, 9]
        low = after[c, :, 0, :] + rim[grid, 0] * halo[grid, k, 0, c]
        high = after[c, :, 15, :] + rim[grid, 1] * halo[grid, k, 1, c]
        after[c, :, 0, :] = low
        after[c, :, 15, :] = high
        if k < SWEEPS - 1:
            edge[grid, k + 1, 0, c] = high
            edge[grid, k + 1, 1, c] = low


def kernel(*refs):
    (
        bg_vel_hbm, nb_vel_hbm, bg_source_hbm, nb_source_hbm, bg_inertia_hbm, nb_inertia_hbm,
        bg_cells_hbm, bg_weights_hbm, nb_cells_hbm, nb_weights_hbm, nb_rec_hbm, bg_rec_hbm,
        bg_out, nb_out,
        bg_vel, nb_vel, bg_source, nb_source, bg_inertia, nb_inertia,
        bg_cells, bg_weights, nb_cells, nb_weights, nb_rec, bg_rec,
        high, low, low8, total,
        bg_sent, nb_sent, bg_held, nb_held, to_near, to_back, bg_run, nb_run,
        bg_frozen, nb_frozen, bg_coef, nb_coef, bg_rhs, nb_rhs, edge, halo, rim,
        load_sems, near_sems, back_sems, send_sems, recv_sems,
    ) = refs
    g = lax.axis_index("grp")
    s = lax.axis_index("sub")

    hbm = refs[:12]
    vmem = refs[14:26]
    loads = [
        pltpu.make_async_copy(hbm[n], vmem[n], load_sems.at[n]) for n in range(12)
    ]
    for n in (0, 6, 7, 1, 8, 9, 10, 11, 2, 3, 4, 5):
        loads[n].start()

    barrier = pltpu.get_barrier_semaphore()

    for offset in range(1, 8):
        pl.semaphore_signal(
            barrier, inc=1, device_id=((g + offset) % 8, s), device_id_type=MESH
        )
    for offset in range(1, 16):
        pl.semaphore_signal(
            barrier, inc=1, device_id=(g, (s + offset) % 16), device_id_type=MESH
        )
    for c in range(3):
        nb_run[0, c, 0] = jnp.zeros((16, 256), F32)
        nb_run[0, c, 9] = jnp.zeros((16, 256), F32)

    near = Exchange(bg_sent, bg_held, to_near, near_sems, g, s)
    back = Exchange(nb_sent, nb_held, to_back, back_sems, g, s)
    for n in (0, 6, 7):
        loads[n].wait()
    interpolate(bg_vel, bg_cells, bg_weights, bg_sent, (high, low, low8), lambda i: None)
    for n in (1, 8, 9):
        loads[n].wait()
    pl.semaphore_wait(barrier, 22)
    near.first_hop()
    interpolate(nb_vel, nb_cells, nb_weights, nb_sent, (high, low, low8), near.second_hop)
    for n in (10, 11, 2, 3, 4, 5):
        loads[n].wait()
    back.first_hop()
    near.arrive()
    overwrite(nb_vel, nb_rec, to_near, nb_run.at[0], nb_frozen, total, back.second_hop)

    copies = []

    def exchange(grid, k, velocity):
        new = halo_copies(grid, k, velocity, edge, halo, send_sems, recv_sems, g, s)
        for copy in new:
            copy.start()
        copies.extend(new)
        return new

    fill_edges(1, 0, nb_run, edge)
    nb_moving = exchange(1, 0, nb_run)
    back.arrive()
    overwrite(bg_vel, bg_rec, to_back, bg_run.at[0], bg_frozen, total, lambda i: None)
    fill_edges(0, 0, bg_run, edge)
    moving = [exchange(0, 0, bg_run), nb_moving]

    runs = (bg_run, nb_run)
    outs = (bg_out, nb_out)
    coefs = (bg_coef, nb_coef)
    sides = (bg_rhs, nb_rhs)
    fields = ((bg_source, bg_inertia, bg_frozen), (nb_source, nb_inertia, nb_frozen))
    for k in range(SWEEPS):
        for grid in (1, 0):
            run, coef, rhs = runs[grid], coefs[grid], sides[grid]
            now = run.at[k]
            after = run.at[k + 1, :, pl.ds(1, 8)] if k < SWEEPS - 1 else outs[grid]
            if k == 0:
                for copy in moving[grid]:
                    copy.wait_recv()
                assemble(grid, run, halo, *fields[grid], coef, rhs, rim, g, s)
            inner(now, coef, rhs, after)
            if k > 0:
                for copy in moving[grid]:
                    copy.wait_recv()
            outer(grid, k, now, halo, coef, rim, after, edge)
            if k < SWEEPS - 1:
                moving[grid] = exchange(grid, k + 1, run)

    near.finish()
    back.finish()
    for copy in copies:
        copy.wait_send()


def body(*args):
    out = jax.ShapeDtypeStruct((3, 8, 16, 256), F32)
    vmem = pltpu.VMEM
    return pl.pallas_call(
        kernel,
        out_shape=(out, out),
        in_specs=[pl.BlockSpec(memory_space=pl.ANY)] * 12,
        out_specs=[pl.BlockSpec(memory_space=vmem)] * 2,
        scratch_shapes=[vmem(a.shape, a.dtype) for a in args]
        + [
            vmem((768, 256), BF),
            vmem((768, 256), BF),
            vmem((768, 256), F8),
            vmem((384, 256), F32),
            vmem((8, 16, 4, 128), F32),
            vmem((8, 16, 4, 128), F32),
            vmem((8, 16, 4, 128), F32),
            vmem((8, 16, 4, 128), F32),
            vmem((16, 8, 4, 128), F32),
            vmem((16, 8, 4, 128), F32),
            vmem((SWEEPS, 3, 10, 16, 256), F32),
            vmem((SWEEPS, 3, 10, 16, 256), F32),
            vmem((8, 16, 256), F32),
            vmem((8, 16, 256), F32),
            vmem((6, 8, 16, 256), F32),
            vmem((6, 8, 16, 256), F32),
            vmem((3, 8, 16, 256), F32),
            vmem((3, 8, 16, 256), F32),
            vmem((2, SWEEPS, 2, 3, 8, 256), F32),
            vmem((2, SWEEPS, 2, 3, 8, 256), F32),
            vmem((2, 2, 8, 256), F32),
            pltpu.SemaphoreType.DMA((12,)),
            pltpu.SemaphoreType.DMA((4,)),
            pltpu.SemaphoreType.DMA((4,)),
            pltpu.SemaphoreType.DMA((2, SWEEPS, 4)),
            pltpu.SemaphoreType.DMA((2, SWEEPS, 4)),
        ],
        compiler_params=pltpu.CompilerParams(
            collective_id=0, has_side_effects=True, vmem_limit_bytes=63 * 2**20
        ),
        name="overset",
    )(*args)


def solution(mesh):
    return jax.shard_map(
        body,
        mesh=mesh,
        in_specs=(
            P(None, "grp", "sub", None),
            P(None, "grp", "sub", None),
            P(None, "grp", "sub", None),
            P(None, "grp", "sub", None),
            P("grp", "sub", None),
            P("grp", "sub", None),
            P(("grp", "sub"), None, None),
            P(("grp", "sub"), None, None, None),
            P(("grp", "sub"), None, None),
            P(("grp", "sub"), None, None, None),
            P(("grp", "sub"), None, None),
            P(("grp", "sub"), None, None),
        ),
        out_specs=(P(None, "grp", "sub", None), P(None, "grp", "sub", None)),
        check_vma=False,
    )
```

```python
import functools

import jax
import jax.numpy as jnp
from jax import lax
from jax.experimental import pallas as pl
from jax.experimental.pallas import tpu as pltpu
from jax.sharding import PartitionSpec as P

BF = jnp.bfloat16
F32 = jnp.float32
F8 = jnp.float8_e4m3fn
LOW = 256.0
TINY = 1e-30
MESH = pl.DeviceIdType.MESH
SWEEPS = 4
HOP_STEP = 7


def split(x):
    hi = x.astype(BF)
    lo = ((x - hi.astype(F32)) * LOW).astype(BF)
    return hi, lo


def iota(shape, dim):
    return lax.broadcasted_iota(jnp.int32, shape, dim)


def scales(peak):
    peak = jnp.maximum(jnp.max(jnp.max(peak, axis=0, keepdims=True), axis=1, keepdims=True), 1e-30)
    return 4.0 / peak, peak * 0.25


def build_table(field, high, low, low8):
    peak = jnp.maximum(jnp.maximum(jnp.abs(field[0]), jnp.abs(field[1])), jnp.abs(field[2]))
    scale, back = scales(peak.reshape(128, 256))
    for c in range(3):
        here = field[c].reshape(128, 256) * scale
        for zc, x in enumerate((here, pltpu.roll(here, 255, 1))):
            hi, lo = split(x)
            for xx in range(8):
                at = xx * 96 + zc * 48 + c * 16
                high[at : at + 16, :] = hi[xx * 16 : xx * 16 + 16]
                low[at : at + 16, :] = lo[xx * 16 : xx * 16 + 16]
    low8[...] = low[...].astype(F8)
    return back


def interpolate_tile(t, cells, weights, out, high, low8, back):
    z_iota = iota((256, 128), 0).astype(F32).astype(BF)
    y_iota = iota((16, 128), 0)
    tile = cells[0, pl.ds(pl.multiple_of(t * 8, 8), 8), :]
    z_tile = (tile & 255).astype(F32).astype(BF)
    y_tile = (tile >> 8) & 15
    x_tile = tile >> 12
    for pair in range(4):
        hot = [
            jnp.where(z_iota == z_tile[s : s + 1, :], jnp.ones((), BF), jnp.zeros((), BF))
            for s in (2 * pair, 2 * pair + 1)
        ]
        hot = jnp.concatenate(hot, axis=1)
        hot8 = (hot * (1.0 / LOW)).astype(F8)
        got = jnp.dot(high[...], hot, preferred_element_type=F32)
        got = got + jnp.dot(low8[...], hot8, preferred_element_type=F32)
        for half in range(2):
            s = 2 * pair + half
            w = weights[0, t * 8 + s]
            y_row = y_tile[s : s + 1, :]
            x_row = jnp.broadcast_to(x_tile[s : s + 1, :], (16, 128))
            y_here = y_iota == y_row
            y_next = y_iota == y_row + 1
            by_y = {}
            for a in range(2):
                for zc in range(2):
                    k = 4 * a + zc
                    by_y[a, zc] = jnp.where(
                        y_here, w[k : k + 1, :], jnp.where(y_next, w[k + 2 : k + 3, :], 0.0)
                    )
            acc = [None] * 3
            before = None
            for xx in range(8):
                here = x_row == xx if xx < 7 else None
                for zc in range(2):
                    coef = None
                    if before is not None:
                        coef = jnp.where(before, by_y[1, zc], 0.0)
                    if here is not None:
                        coef = jnp.where(here, by_y[0, zc], 0.0 if coef is None else coef)
                    for c in range(3):
                        at = xx * 96 + zc * 48 + c * 16
                        term = coef * got[at : at + 16, half * 128 : half * 128 + 128]
                        acc[c] = term if acc[c] is None else acc[c] + term
                before = here
            for c in range(3):
                out[t // 2, (t % 2) * 8 + s, c, :] = jnp.sum(acc[c], axis=0) * back[0]


def interpolate(field, cells, weights, sent, tables, beside):
    high, low, low8 = tables
    back = build_table(field, high, low, low8)

    def step(i, carry):
        beside(i)
        interpolate_tile(i, cells, weights, sent, high, low8, back)
        return carry

    lax.fori_loop(0, 16, step, 0)


class Exchange:
    def __init__(self, sent, held, came, sems, g, s):
        self.sent, self.held, self.came, self.sems, self.g, self.s = sent, held, came, sems, g, s

    def across(self, offset):
        peer = (self.g + offset) % 8
        return pltpu.make_async_remote_copy(
            src_ref=self.sent.at[peer],
            dst_ref=self.held.at[self.g],
            send_sem=self.sems.at[0],
            recv_sem=self.sems.at[1],
            device_id=(peer, self.s),
            device_id_type=MESH,
        )

    def along(self, offset):
        peer = (self.s + offset) % 16
        return pltpu.make_async_remote_copy(
            src_ref=self.held.at[:, peer],
            dst_ref=self.came.at[self.s],
            send_sem=self.sems.at[2],
            recv_sem=self.sems.at[3],
            device_id=(self.g, peer),
            device_id_type=MESH,
        )

    def all_across(self):
        return pltpu.make_async_remote_copy(
            src_ref=self.sent.at[pl.ds(0, 7)],
            dst_ref=self.held.at[pl.ds(0, 7)],
            send_sem=self.sems.at[0],
            recv_sem=self.sems.at[1],
            device_id=((self.g + 1) % 8, self.s),
            device_id_type=MESH,
        )

    def all_along(self):
        return pltpu.make_async_remote_copy(
            src_ref=self.came.at[pl.ds(0, 15)],
            dst_ref=self.came.at[pl.ds(0, 15)],
            send_sem=self.sems.at[2],
            recv_sem=self.sems.at[3],
            device_id=(self.g, (self.s + 1) % 16),
            device_id_type=MESH,
        )

    def first_hop(self):
        for offset in (4, 3, 5, 2, 6, 1, 7):
            self.across(offset).start()
        self.held[self.g] = self.sent[self.g]

    def second_hop(self, i):
        @pl.when(i == HOP_STEP)
        def _():
            self.all_across().wait_recv()
            for offset in range(1, 16):
                self.along(offset).start()
            self.came[self.s] = self.held[:, self.s]

    def arrive(self):
        self.all_along().wait_recv()

    def finish(self):
        self.all_across().wait_send()
        self.all_along().wait_send()


def overwrite(field, receptors, got, start, frozen, total, beside):
    z_iota = iota((256, 128), 0).astype(F32).astype(BF)
    r_iota = iota((128, 128), 0).astype(F32).astype(BF)
    row = iota((4, 128), 0)
    peak = jnp.zeros((4, 128), F32)
    for p in range(16):
        peak = jnp.maximum(peak, jnp.max(jnp.abs(got[p]), axis=0))
    scale, back = scales(jnp.where(row < 3, peak, 0.0))
    one = jnp.ones((), BF)
    zero = jnp.zeros((), BF)
    total[...] = jnp.zeros_like(total)

    def step(i, carry):
        beside(i)
        tile = receptors[0, pl.ds(pl.multiple_of(i * 8, 8), 8), :]
        z_tile = (tile & 255).astype(F32).astype(BF)
        r_tile = (tile >> 8).astype(F32).astype(BF)
        for half in range(2):
            hots = []
            highs = []
            lows = []
            for s in range(4 * half, 4 * half + 4):
                hots.append(jnp.where(z_iota == z_tile[s : s + 1, :], one, zero))
                mine = r_iota == r_tile[s : s + 1, :]
                hi, lo = split(got[(i % 2) * 8 + s, i // 2] * scale)
                hi = hi.astype(F32)
                hi = jnp.where((hi == 0.0) & (row == 0), TINY, hi).astype(BF)
                for rows, part in ((highs, hi), (lows, lo)):
                    picked = [jnp.where(mine, part[c : c + 1, :], zero) for c in range(3)]
                    rows.append(jnp.concatenate(picked, axis=0))
            hot = jnp.concatenate(hots, axis=1)
            hot8 = (hot * (1.0 / LOW)).astype(F8)
            over_slots = (((1,), (1,)), ((), ()))
            total[...] += lax.dot_general(
                jnp.concatenate(highs, axis=1), hot, over_slots, preferred_element_type=F32
            ) + lax.dot_general(
                jnp.concatenate(lows, axis=1).astype(F8),
                hot8,
                over_slots,
                preferred_element_type=F32,
            )
        return carry

    lax.fori_loop(0, 16, step, 0)
    mask = total[0:128, :] != 0.0
    frozen[...] = jnp.where(mask, 1.0, 0.0).reshape(8, 16, 256)
    for c in range(3):
        value = total[c * 128 : c * 128 + 128, :]
        if c == 0:
            value = jnp.where(jnp.abs(value) < 2.0 * TINY, 0.0, value)
        old = field[c].reshape(128, 256)
        start[c, 1:9] = jnp.where(mask, value * back, old).reshape(8, 16, 256)


def halo_copies(grid, k, velocity, edge, halo, send_sems, recv_sems, g, s):
    north, south = (s + 1) % 16, (s + 15) % 16
    plan = [
        (edge.at[grid, k, 0], halo.at[grid, k, 0], (g, north)),
        (edge.at[grid, k, 1], halo.at[grid, k, 1], (g, south)),
    ]
    if grid == 0:
        plan += [
            (velocity.at[k, :, 8], velocity.at[k, :, 0], ((g + 1) % 8, s)),
            (velocity.at[k, :, 1], velocity.at[k, :, 9], ((g + 7) % 8, s)),
        ]
    return [
        pltpu.make_async_remote_copy(
            src_ref=source,
            dst_ref=target,
            send_sem=send_sems.at[grid, k, n],
            recv_sem=recv_sems.at[grid, k, n],
            device_id=device,
            device_id_type=MESH,
        )
        for n, (source, target, device) in enumerate(plan)
    ]


def fill_edges(grid, k, velocity, edge):
    for c in range(3):
        edge[grid, k, 0, c] = velocity[k, c, 1:9, 15, :]
        edge[grid, k, 1, c] = velocity[k, c, 1:9, 0, :]


def shifted(plane, low, high):
    y = iota((16, 256), 0)
    after_y = jnp.where(y == 15, high, pltpu.roll(plane, 15, 0))
    before_y = jnp.where(y == 0, low, pltpu.roll(plane, 1, 0))
    return after_y, before_y, pltpu.roll(plane, 255, 1), pltpu.roll(plane, 1, 1)


def assemble(grid, velocity, halo, source, inertia, frozen, coef, rhs, rim, g, s):
    y = iota((16, 256), 0)
    z = iota((16, 256), 1)
    y_low = jnp.where(s > 0, 1.0, 0.0)
    y_high = jnp.where(s < 15, 1.0, 0.0)

    def face(middle, other, sign):
        return 1.0 + jnp.maximum(sign * (middle + other), 0.0)

    def step(x, carry):
        u, v, w = (velocity[0, c, x + 1] for c in range(3))
        if grid == 0:
            x_low = jnp.where((x > 0) | (g > 0), 1.0, 0.0)
            x_high = jnp.where((x < 7) | (g < 7), 1.0, 0.0)
        else:
            x_low = jnp.where(x > 0, 1.0, 0.0)
            x_high = jnp.where(x < 7, 1.0, 0.0)
        low = halo[grid, 0, 0, 1, pl.ds(x, 1), :] * y_low
        high = halo[grid, 0, 1, 1, pl.ds(x, 1), :] * y_high
        v_after, v_before, _, _ = shifted(v, low, high)
        w_after = jnp.where(z == 255, 0.0, pltpu.roll(w, 255, 1))
        w_before = jnp.where(z == 0, 0.0, pltpu.roll(w, 1, 1))
        faces = [
            face(u, velocity[0, 0, x + 2] * x_high, -0.5),
            face(u, velocity[0, 0, x] * x_low, 0.5),
            face(v, v_after, -0.5),
            face(v, v_before, 0.5),
            face(w, w_after, -0.5),
            face(w, w_before, 0.5),
        ]
        weight = inertia[x]
        diagonal = weight
        for f in faces:
            diagonal = diagonal + f
        inverse = 1.0 / diagonal
        stuck = frozen[x] > 0.5
        live = jnp.where(stuck, 0.0, inverse)
        faces = [f * live for f in faces]
        coef[0, x] = faces[0] * x_high
        coef[1, x] = faces[1] * x_low
        coef[2, x] = faces[2]
        coef[3, x] = faces[3]
        coef[4, x] = jnp.where(z == 255, 0.0, faces[4])
        coef[5, x] = jnp.where(z == 0, 0.0, faces[5])
        for c, start in enumerate((u, v, w)):
            right = (source[c, x] + weight * start) * inverse
            rhs[c, x] = jnp.where(stuck, start, right)
        return carry

    lax.fori_loop(0, 8, step, 0)
    rim[grid, 0] = coef[3, :, 0, :] * y_low
    rim[grid, 1] = coef[2, :, 15, :] * y_high
    coef[3, :, 0, :] = jnp.zeros((8, 256), F32)
    coef[2, :, 15, :] = jnp.zeros((8, 256), F32)


def inner(now, coef, rhs, after):
    for x in range(8):
        for c in range(3):
            plane = now[c, x + 1]
            total = rhs[c, x]
            if x < 7:
                total = total + coef[0, x] * now[c, x + 2]
            if x > 0:
                total = total + coef[1, x] * now[c, x]
            total = total + coef[2, x] * pltpu.roll(plane, 15, 0)
            total = total + coef[3, x] * pltpu.roll(plane, 1, 0)
            total = total + coef[4, x] * pltpu.roll(plane, 255, 1)
            total = total + coef[5, x] * pltpu.roll(plane, 1, 1)
            after[c, x] = total


def outer(grid, k, now, halo, coef, rim, after, edge):
    for c in range(3):
        if grid == 0:
            after[c, 0] = after[c, 0] + coef[1, 0] * now[c, 0]
            after[c, 7] = after[c, 7] + coef[0, 7] * now[c, 9]
        low = after[c, :, 0, :] + rim[grid, 0] * halo[grid, k, 0, c]
        high = after[c, :, 15, :] + rim[grid, 1] * halo[grid, k, 1, c]
        after[c, :, 0, :] = low
        after[c, :, 15, :] = high
        if k < SWEEPS - 1:
            edge[grid, k + 1, 0, c] = high
            edge[grid, k + 1, 1, c] = low


def kernel(*refs):
    (
        bg_vel_hbm, nb_vel_hbm, bg_source_hbm, nb_source_hbm, bg_inertia_hbm, nb_inertia_hbm,
        bg_cells_hbm, bg_weights_hbm, nb_cells_hbm, nb_weights_hbm, nb_rec_hbm, bg_rec_hbm,
        bg_out, nb_out,
        bg_vel, nb_vel, bg_source, nb_source, bg_inertia, nb_inertia,
        bg_cells, bg_weights, nb_cells, nb_weights, nb_rec, bg_rec,
        high, low, low8, total,
        bg_sent, nb_sent, bg_held, nb_held, to_near, to_back, bg_run, nb_run,
        bg_frozen, nb_frozen, bg_coef, nb_coef, bg_rhs, nb_rhs, edge, halo, rim,
        load_sems, near_sems, back_sems, send_sems, recv_sems,
    ) = refs
    g = lax.axis_index("grp")
    s = lax.axis_index("sub")

    hbm = refs[:12]
    vmem = refs[14:26]
    loads = [
        pltpu.make_async_copy(hbm[n], vmem[n], load_sems.at[n]) for n in range(12)
    ]
    for n in (0, 6, 7):
        loads[n].start()

    barrier = pltpu.get_barrier_semaphore()

    for c in range(3):
        for end in (0, 9):
            nb_run[0, c, end] = jnp.zeros((16, 256), F32)
            for k in range(SWEEPS):
                bg_run[k, c, end] = jnp.zeros((16, 256), F32)
    halo[...] = jnp.zeros_like(halo)
    for offset in range(1, 8):
        pl.semaphore_signal(
            barrier, inc=1, device_id=((g + offset) % 8, s), device_id_type=MESH
        )
    for offset in range(1, 16):
        pl.semaphore_signal(
            barrier, inc=1, device_id=(g, (s + offset) % 16), device_id_type=MESH
        )

    near = Exchange(bg_sent, bg_held, to_near, near_sems, g, s)
    back = Exchange(nb_sent, nb_held, to_back, back_sems, g, s)
    for n in (0, 6, 7):
        loads[n].wait()
    for n in (1, 8, 9, 10, 11, 2, 3, 4, 5):
        loads[n].start()
    interpolate(bg_vel, bg_cells, bg_weights, bg_sent, (high, low, low8), lambda i: None)
    for n in (1, 8, 9):
        loads[n].wait()
    pl.semaphore_wait(barrier, 22)
    near.first_hop()
    interpolate(nb_vel, nb_cells, nb_weights, nb_sent, (high, low, low8), near.second_hop)
    for n in (10, 11, 2, 3, 4, 5):
        loads[n].wait()
    back.first_hop()
    near.arrive()
    overwrite(nb_vel, nb_rec, to_near, nb_run.at[0], nb_frozen, total, back.second_hop)

    goes = (s < 15, s > 0, g < 7, g > 0)
    comes = (s > 0, s < 15, g > 0, g < 7)
    copies = []

    def each(conditions, new, act):
        for condition, copy in zip(conditions, new):
            pl.when(condition)(functools.partial(act, copy))

    def exchange(grid, k, velocity):
        new = halo_copies(grid, k, velocity, edge, halo, send_sems, recv_sems, g, s)
        each(goes, new, lambda copy: copy.start())
        copies.append(new)
        return new

    fill_edges(1, 0, nb_run, edge)
    nb_moving = exchange(1, 0, nb_run)
    back.arrive()
    overwrite(bg_vel, bg_rec, to_back, bg_run.at[0], bg_frozen, total, lambda i: None)
    fill_edges(0, 0, bg_run, edge)
    moving = [exchange(0, 0, bg_run), nb_moving]

    runs = (bg_run, nb_run)
    outs = (bg_out, nb_out)
    coefs = (bg_coef, nb_coef)
    sides = (bg_rhs, nb_rhs)
    fields = ((bg_source, bg_inertia, bg_frozen), (nb_source, nb_inertia, nb_frozen))
    for k in range(SWEEPS):
        for grid in (1, 0):
            run, coef, rhs = runs[grid], coefs[grid], sides[grid]
            now = run.at[k]
            after = run.at[k + 1, :, pl.ds(1, 8)] if k < SWEEPS - 1 else outs[grid]
            if k == 0:
                each(comes, moving[grid], lambda copy: copy.wait_recv())
                assemble(grid, run, halo, *fields[grid], coef, rhs, rim, g, s)
            inner(now, coef, rhs, after)
            if k > 0:
                each(comes, moving[grid], lambda copy: copy.wait_recv())
            outer(grid, k, now, halo, coef, rim, after, edge)
            if k < SWEEPS - 1:
                moving[grid] = exchange(grid, k + 1, run)

    near.finish()
    back.finish()
    for new in copies:
        each(goes, new, lambda copy: copy.wait_send())


def body(*args):
    out = jax.ShapeDtypeStruct((3, 8, 16, 256), F32)
    vmem = pltpu.VMEM
    return pl.pallas_call(
        kernel,
        out_shape=(out, out),
        in_specs=[pl.BlockSpec(memory_space=pl.ANY)] * 12,
        out_specs=[pl.BlockSpec(memory_space=vmem)] * 2,
        scratch_shapes=[vmem(a.shape, a.dtype) for a in args]
        + [
            vmem((768, 256), BF),
            vmem((768, 256), BF),
            vmem((768, 256), F8),
            vmem((384, 256), F32),
            vmem((8, 16, 4, 128), F32),
            vmem((8, 16, 4, 128), F32),
            vmem((8, 16, 4, 128), F32),
            vmem((8, 16, 4, 128), F32),
            vmem((16, 8, 4, 128), F32),
            vmem((16, 8, 4, 128), F32),
            vmem((SWEEPS, 3, 10, 16, 256), F32),
            vmem((SWEEPS, 3, 10, 16, 256), F32),
            vmem((8, 16, 256), F32),
            vmem((8, 16, 256), F32),
            vmem((6, 8, 16, 256), F32),
            vmem((6, 8, 16, 256), F32),
            vmem((3, 8, 16, 256), F32),
            vmem((3, 8, 16, 256), F32),
            vmem((2, SWEEPS, 2, 3, 8, 256), F32),
            vmem((2, SWEEPS, 2, 3, 8, 256), F32),
            vmem((2, 2, 8, 256), F32),
            pltpu.SemaphoreType.DMA((12,)),
            pltpu.SemaphoreType.DMA((4,)),
            pltpu.SemaphoreType.DMA((4,)),
            pltpu.SemaphoreType.DMA((2, SWEEPS, 4)),
            pltpu.SemaphoreType.DMA((2, SWEEPS, 4)),
        ],
        compiler_params=pltpu.CompilerParams(
            collective_id=0, has_side_effects=True, vmem_limit_bytes=63 * 2**20
        ),
        name="overset",
    )(*args)


def solution(mesh):
    return jax.shard_map(
        body,
        mesh=mesh,
        in_specs=(
            P(None, "grp", "sub", None),
            P(None, "grp", "sub", None),
            P(None, "grp", "sub", None),
            P(None, "grp", "sub", None),
            P("grp", "sub", None),
            P("grp", "sub", None),
            P(("grp", "sub"), None, None),
            P(("grp", "sub"), None, None, None),
            P(("grp", "sub"), None, None),
            P(("grp", "sub"), None, None, None),
            P(("grp", "sub"), None, None),
            P(("grp", "sub"), None, None),
        ),
        out_specs=(P(None, "grp", "sub", None), P(None, "grp", "sub", None)),
        check_vma=False,
    )
```

```python
import functools

import jax
import jax.numpy as jnp
from jax import lax
from jax.experimental import pallas as pl
from jax.experimental.pallas import tpu as pltpu
from jax.sharding import PartitionSpec as P

BF = jnp.bfloat16
F32 = jnp.float32
F8 = jnp.float8_e4m3fn
REACH = 1024.0
TINY = 1e-30
MESH = pl.DeviceIdType.MESH
SWEEPS = 4


def split(x):
    hi = x.astype(BF)
    lo = (x - hi.astype(F32)).astype(BF)
    return hi, lo


def iota(shape, dim):
    return lax.broadcasted_iota(jnp.int32, shape, dim)


def scales(peak):
    peak = jnp.maximum(jnp.max(jnp.max(peak, axis=0, keepdims=True), axis=1, keepdims=True), 1e-30)
    return REACH / peak, peak * (1.0 / REACH)


def build_table(field, high, low, low8):
    peak = jnp.maximum(jnp.maximum(jnp.abs(field[0]), jnp.abs(field[1])), jnp.abs(field[2]))
    scale, back = scales(peak.reshape(128, 256))
    for c in range(3):
        here = field[c].reshape(128, 256) * scale
        for zc, x in enumerate((here, pltpu.roll(here, 255, 1))):
            hi, lo = split(x)
            for xx in range(8):
                at = xx * 96 + zc * 48 + c * 16
                high[at : at + 16, :] = hi[xx * 16 : xx * 16 + 16]
                low[at : at + 16, :] = lo[xx * 16 : xx * 16 + 16]
    low8[...] = low[...].astype(F8)
    return back


def interpolate_tile(t, cells, weights, out, high, low8, back):
    z_iota = iota((256, 128), 0).astype(F32).astype(BF)
    y_iota = iota((16, 128), 0)
    tile = cells[0, pl.ds(pl.multiple_of(t * 8, 8), 8), :]
    z_tile = (tile & 255).astype(F32).astype(BF)
    y_tile = (tile >> 8) & 15
    x_tile = tile >> 12
    for pair in range(4):
        hot = [
            jnp.where(z_iota == z_tile[s : s + 1, :], jnp.ones((), BF), jnp.zeros((), BF))
            for s in (2 * pair, 2 * pair + 1)
        ]
        hot = jnp.concatenate(hot, axis=1)
        hot8 = hot.astype(F8)
        got = jnp.dot(high[...], hot, preferred_element_type=F32)
        got = got + jnp.dot(low8[...], hot8, preferred_element_type=F32)
        for half in range(2):
            s = 2 * pair + half
            w = weights[0, t * 8 + s]
            y_row = y_tile[s : s + 1, :]
            x_row = jnp.broadcast_to(x_tile[s : s + 1, :], (16, 128))
            y_here = y_iota == y_row
            y_next = y_iota == y_row + 1
            by_y = {}
            for a in range(2):
                for zc in range(2):
                    k = 4 * a + zc
                    by_y[a, zc] = jnp.where(
                        y_here, w[k : k + 1, :], jnp.where(y_next, w[k + 2 : k + 3, :], 0.0)
                    )
            acc = [None] * 3
            before = None
            for xx in range(8):
                here = x_row == xx if xx < 7 else None
                for zc in range(2):
                    coef = None
                    if before is not None:
                        coef = jnp.where(before, by_y[1, zc], 0.0)
                    if here is not None:
                        coef = jnp.where(here, by_y[0, zc], 0.0 if coef is None else coef)
                    for c in range(3):
                        at = xx * 96 + zc * 48 + c * 16
                        term = coef * got[at : at + 16, half * 128 : half * 128 + 128]
                        acc[c] = term if acc[c] is None else acc[c] + term
                before = here
            for c in range(3):
                out[t // 2, (t % 2) * 8 + s, c, :] = jnp.sum(acc[c], axis=0) * back[0]


def interpolate(field, cells, weights, sent, tables, beside):
    high, low, low8 = tables
    back = build_table(field, high, low, low8)

    def step(i, carry):
        beside(i)
        interpolate_tile(i, cells, weights, sent, high, low8, back)
        return carry

    lax.fori_loop(0, 16, step, 0)


class Exchange:
    def __init__(self, sent, held, came, sems, g, s, turn):
        self.sent, self.held, self.came, self.sems, self.g, self.s = sent, held, came, sems, g, s
        self.turn = turn

    def across(self, offset):
        peer = (self.g + offset) % 8
        return pltpu.make_async_remote_copy(
            src_ref=self.sent.at[peer],
            dst_ref=self.held.at[self.g],
            send_sem=self.sems.at[0],
            recv_sem=self.sems.at[1],
            device_id=(peer, self.s),
            device_id_type=MESH,
        )

    def along(self, offset):
        peer = (self.s + offset) % 16
        return pltpu.make_async_remote_copy(
            src_ref=self.held.at[:, peer],
            dst_ref=self.came.at[self.s],
            send_sem=self.sems.at[2],
            recv_sem=self.sems.at[3],
            device_id=(self.g, peer),
            device_id_type=MESH,
        )

    def all_across(self):
        return pltpu.make_async_remote_copy(
            src_ref=self.sent.at[pl.ds(0, 7)],
            dst_ref=self.held.at[pl.ds(0, 7)],
            send_sem=self.sems.at[0],
            recv_sem=self.sems.at[1],
            device_id=((self.g + 1) % 8, self.s),
            device_id_type=MESH,
        )

    def all_along(self):
        return pltpu.make_async_remote_copy(
            src_ref=self.came.at[pl.ds(0, 15)],
            dst_ref=self.came.at[pl.ds(0, 15)],
            send_sem=self.sems.at[2],
            recv_sem=self.sems.at[3],
            device_id=(self.g, (self.s + 1) % 16),
            device_id_type=MESH,
        )

    def first_hop(self):
        for offset in (4, 3, 5, 2, 6, 1, 7):
            self.across(offset).start()
        self.held[self.g] = self.sent[self.g]

    def second_hop(self, i):
        @pl.when(i == self.turn)
        def _():
            self.all_across().wait_recv()
            for offset in range(1, 16):
                self.along(offset).start()
            self.came[self.s] = self.held[:, self.s]

    def arrive(self):
        self.all_along().wait_recv()

    def finish(self):
        self.all_across().wait_send()
        self.all_along().wait_send()


def overwrite(field, receptors, got, start, frozen, total, beside):
    z_iota = iota((256, 128), 0).astype(F32).astype(BF)
    r_iota = iota((128, 128), 0).astype(F32).astype(BF)
    row = iota((4, 128), 0)
    peak = jnp.zeros((4, 128), F32)
    for p in range(16):
        peak = jnp.maximum(peak, jnp.max(jnp.abs(got[p]), axis=0))
    scale, back = scales(jnp.where(row < 3, peak, 0.0))
    one = jnp.ones((), BF)
    zero = jnp.zeros((), BF)
    total[...] = jnp.zeros_like(total)

    def step(i, carry):
        beside(i)
        tile = receptors[0, pl.ds(pl.multiple_of(i * 8, 8), 8), :]
        z_tile = (tile & 255).astype(F32).astype(BF)
        r_tile = (tile >> 8).astype(F32).astype(BF)
        for half in range(2):
            hots = []
            highs = []
            lows = []
            for s in range(4 * half, 4 * half + 4):
                hots.append(jnp.where(z_iota == z_tile[s : s + 1, :], one, zero))
                mine = r_iota == r_tile[s : s + 1, :]
                hi, lo = split(got[(i % 2) * 8 + s, i // 2] * scale)
                hi = hi.astype(F32)
                hi = jnp.where((hi == 0.0) & (row == 0), TINY, hi).astype(BF)
                for rows, part in ((highs, hi), (lows, lo)):
                    picked = [jnp.where(mine, part[c : c + 1, :], zero) for c in range(3)]
                    rows.append(jnp.concatenate(picked, axis=0))
            hot = jnp.concatenate(hots, axis=1)
            hot8 = hot.astype(F8)
            over_slots = (((1,), (1,)), ((), ()))
            total[...] += lax.dot_general(
                jnp.concatenate(highs, axis=1), hot, over_slots, preferred_element_type=F32
            ) + lax.dot_general(
                jnp.concatenate(lows, axis=1).astype(F8),
                hot8,
                over_slots,
                preferred_element_type=F32,
            )
        return carry

    lax.fori_loop(0, 16, step, 0)
    mask = total[0:128, :] != 0.0
    frozen[...] = jnp.where(mask, 1.0, 0.0).reshape(8, 16, 256)
    for c in range(3):
        value = total[c * 128 : c * 128 + 128, :]
        if c == 0:
            value = jnp.where(jnp.abs(value) < 2.0 * TINY, 0.0, value)
        old = field[c].reshape(128, 256)
        start[c, 1:9] = jnp.where(mask, value * back, old).reshape(8, 16, 256)


def halo_copies(grid, k, velocity, edge, halo, send_sems, recv_sems, g, s):
    north, south = (s + 1) % 16, (s + 15) % 16
    plan = [
        (edge.at[grid, k, 0], halo.at[grid, k, 0], (g, north)),
        (edge.at[grid, k, 1], halo.at[grid, k, 1], (g, south)),
    ]
    if grid == 0:
        plan += [
            (velocity.at[k, :, 8], velocity.at[k, :, 0], ((g + 1) % 8, s)),
            (velocity.at[k, :, 1], velocity.at[k, :, 9], ((g + 7) % 8, s)),
        ]
    return [
        pltpu.make_async_remote_copy(
            src_ref=source,
            dst_ref=target,
            send_sem=send_sems.at[grid, k, n],
            recv_sem=recv_sems.at[grid, k, n],
            device_id=device,
            device_id_type=MESH,
        )
        for n, (source, target, device) in enumerate(plan)
    ]


def fill_edges(grid, k, velocity, edge):
    for c in range(3):
        edge[grid, k, 0, c] = velocity[k, c, 1:9, 15, :]
        edge[grid, k, 1, c] = velocity[k, c, 1:9, 0, :]


def shifted(plane, low, high):
    y = iota((16, 256), 0)
    after_y = jnp.where(y == 15, high, pltpu.roll(plane, 15, 0))
    before_y = jnp.where(y == 0, low, pltpu.roll(plane, 1, 0))
    return after_y, before_y, pltpu.roll(plane, 255, 1), pltpu.roll(plane, 1, 1)


def assemble(grid, velocity, halo, source, inertia, frozen, coef, rhs, rim, g, s):
    y = iota((16, 256), 0)
    z = iota((16, 256), 1)
    y_low = jnp.where(s > 0, 1.0, 0.0)
    y_high = jnp.where(s < 15, 1.0, 0.0)

    def face(middle, other, sign):
        return 1.0 + jnp.maximum(sign * (middle + other), 0.0)

    def step(x, carry):
        u, v, w = (velocity[0, c, x + 1] for c in range(3))
        if grid == 0:
            x_low = jnp.where((x > 0) | (g > 0), 1.0, 0.0)
            x_high = jnp.where((x < 7) | (g < 7), 1.0, 0.0)
        else:
            x_low = jnp.where(x > 0, 1.0, 0.0)
            x_high = jnp.where(x < 7, 1.0, 0.0)
        low = halo[grid, 0, 0, 1, pl.ds(x, 1), :] * y_low
        high = halo[grid, 0, 1, 1, pl.ds(x, 1), :] * y_high
        v_after, v_before, _, _ = shifted(v, low, high)
        w_after = jnp.where(z == 255, 0.0, pltpu.roll(w, 255, 1))
        w_before = jnp.where(z == 0, 0.0, pltpu.roll(w, 1, 1))
        faces = [
            face(u, velocity[0, 0, x + 2] * x_high, -0.5),
            face(u, velocity[0, 0, x] * x_low, 0.5),
            face(v, v_after, -0.5),
            face(v, v_before, 0.5),
            face(w, w_after, -0.5),
            face(w, w_before, 0.5),
        ]
        weight = inertia[x]
        diagonal = weight
        for f in faces:
            diagonal = diagonal + f
        inverse = 1.0 / diagonal
        stuck = frozen[x] > 0.5
        live = jnp.where(stuck, 0.0, inverse)
        faces = [f * live for f in faces]
        coef[0, x] = faces[0] * x_high
        coef[1, x] = faces[1] * x_low
        coef[2, x] = faces[2]
        coef[3, x] = faces[3]
        coef[4, x] = jnp.where(z == 255, 0.0, faces[4])
        coef[5, x] = jnp.where(z == 0, 0.0, faces[5])
        for c, start in enumerate((u, v, w)):
            right = (source[c, x] + weight * start) * inverse
            rhs[c, x] = jnp.where(stuck, start, right)
        return carry

    lax.fori_loop(0, 8, step, 0, unroll=4)
    rim[grid, 0] = coef[3, :, 0, :] * y_low
    rim[grid, 1] = coef[2, :, 15, :] * y_high
    coef[3, :, 0, :] = jnp.zeros((8, 256), F32)
    coef[2, :, 15, :] = jnp.zeros((8, 256), F32)


def inner(now, coef, rhs, after):
    for x in range(8):
        for c in range(3):
            plane = now[c, x + 1]
            total = rhs[c, x]
            if x < 7:
                total = total + coef[0, x] * now[c, x + 2]
            if x > 0:
                total = total + coef[1, x] * now[c, x]
            total = total + coef[2, x] * pltpu.roll(plane, 15, 0)
            total = total + coef[3, x] * pltpu.roll(plane, 1, 0)
            total = total + coef[4, x] * pltpu.roll(plane, 255, 1)
            total = total + coef[5, x] * pltpu.roll(plane, 1, 1)
            after[c, x] = total


def outer(grid, k, now, halo, coef, rim, after, edge):
    for c in range(3):
        if grid == 0:
            after[c, 0] = after[c, 0] + coef[1, 0] * now[c, 0]
            after[c, 7] = after[c, 7] + coef[0, 7] * now[c, 9]
        low = after[c, :, 0, :] + rim[grid, 0] * halo[grid, k, 0, c]
        high = after[c, :, 15, :] + rim[grid, 1] * halo[grid, k, 1, c]
        after[c, :, 0, :] = low
        after[c, :, 15, :] = high
        if k < SWEEPS - 1:
            edge[grid, k + 1, 0, c] = high
            edge[grid, k + 1, 1, c] = low


def kernel(*refs):
    (
        bg_vel_hbm, nb_vel_hbm, bg_source_hbm, nb_source_hbm, bg_inertia_hbm, nb_inertia_hbm,
        bg_cells_hbm, bg_weights_hbm, nb_cells_hbm, nb_weights_hbm, nb_rec_hbm, bg_rec_hbm,
        bg_out, nb_out,
        bg_vel, nb_vel, bg_source, nb_source, bg_inertia, nb_inertia,
        bg_cells, bg_weights, nb_cells, nb_weights, nb_rec, bg_rec,
        high, low, low8, total,
        bg_sent, nb_sent, bg_held, nb_held, to_near, to_back, bg_run, nb_run,
        bg_frozen, nb_frozen, bg_coef, nb_coef, bg_rhs, nb_rhs, edge, halo, rim,
        load_sems, near_sems, back_sems, send_sems, recv_sems,
    ) = refs
    g = lax.axis_index("grp")
    s = lax.axis_index("sub")

    hbm = refs[:12]
    vmem = refs[14:26]
    loads = [
        pltpu.make_async_copy(hbm[n], vmem[n], load_sems.at[n]) for n in range(12)
    ]
    for n in (0, 6, 7):
        loads[n].start()

    barrier = pltpu.get_barrier_semaphore()

    for c in range(3):
        for end in (0, 9):
            nb_run[0, c, end] = jnp.zeros((16, 256), F32)
            for k in range(SWEEPS):
                bg_run[k, c, end] = jnp.zeros((16, 256), F32)
    halo[...] = jnp.zeros_like(halo)
    for offset in range(1, 8):
        pl.semaphore_signal(
            barrier, inc=1, device_id=((g + offset) % 8, s), device_id_type=MESH
        )
    for offset in range(1, 16):
        pl.semaphore_signal(
            barrier, inc=1, device_id=(g, (s + offset) % 16), device_id_type=MESH
        )

    near = Exchange(bg_sent, bg_held, to_near, near_sems, g, s, 7)
    back = Exchange(nb_sent, nb_held, to_back, back_sems, g, s, 5)
    for n in (0, 6, 7):
        loads[n].wait()
    for n in (1, 8, 9, 10, 11, 2, 3, 4, 5):
        loads[n].start()
    interpolate(bg_vel, bg_cells, bg_weights, bg_sent, (high, low, low8), lambda i: None)
    for n in (1, 8, 9):
        loads[n].wait()
    pl.semaphore_wait(barrier, 22)
    near.first_hop()
    interpolate(nb_vel, nb_cells, nb_weights, nb_sent, (high, low, low8), near.second_hop)
    for n in (10, 11, 2, 3, 4, 5):
        loads[n].wait()
    back.first_hop()
    near.arrive()
    overwrite(nb_vel, nb_rec, to_near, nb_run.at[0], nb_frozen, total, back.second_hop)

    goes = (s < 15, s > 0, g < 7, g > 0)
    comes = (s > 0, s < 15, g > 0, g < 7)
    copies = []

    def each(conditions, new, act):
        for condition, copy in zip(conditions, new):
            pl.when(condition)(functools.partial(act, copy))

    def exchange(grid, k, velocity):
        new = halo_copies(grid, k, velocity, edge, halo, send_sems, recv_sems, g, s)
        each(goes, new, lambda copy: copy.start())
        copies.append(new)
        return new

    fill_edges(1, 0, nb_run, edge)
    nb_moving = exchange(1, 0, nb_run)
    back.arrive()
    overwrite(bg_vel, bg_rec, to_back, bg_run.at[0], bg_frozen, total, lambda i: None)
    fill_edges(0, 0, bg_run, edge)
    moving = [exchange(0, 0, bg_run), nb_moving]

    runs = (bg_run, nb_run)
    outs = (bg_out, nb_out)
    coefs = (bg_coef, nb_coef)
    sides = (bg_rhs, nb_rhs)
    fields = ((bg_source, bg_inertia, bg_frozen), (nb_source, nb_inertia, nb_frozen))
    for k in range(SWEEPS):
        for grid in (1, 0):
            run, coef, rhs = runs[grid], coefs[grid], sides[grid]
            now = run.at[k]
            after = run.at[k + 1, :, pl.ds(1, 8)] if k < SWEEPS - 1 else outs[grid]
            if k == 0:
                each(comes, moving[grid], lambda copy: copy.wait_recv())
                assemble(grid, run, halo, *fields[grid], coef, rhs, rim, g, s)
            inner(now, coef, rhs, after)
            if k > 0:
                each(comes, moving[grid], lambda copy: copy.wait_recv())
            outer(grid, k, now, halo, coef, rim, after, edge)
            if k < SWEEPS - 1:
                moving[grid] = exchange(grid, k + 1, run)

    near.finish()
    back.finish()
    for new in copies:
        each(goes, new, lambda copy: copy.wait_send())


def body(*args):
    out = jax.ShapeDtypeStruct((3, 8, 16, 256), F32)
    vmem = pltpu.VMEM
    return pl.pallas_call(
        kernel,
        out_shape=(out, out),
        in_specs=[pl.BlockSpec(memory_space=pl.ANY)] * 12,
        out_specs=[pl.BlockSpec(memory_space=vmem)] * 2,
        scratch_shapes=[vmem(a.shape, a.dtype) for a in args]
        + [
            vmem((768, 256), BF),
            vmem((768, 256), BF),
            vmem((768, 256), F8),
            vmem((384, 256), F32),
            vmem((8, 16, 4, 128), F32),
            vmem((8, 16, 4, 128), F32),
            vmem((8, 16, 4, 128), F32),
            vmem((8, 16, 4, 128), F32),
            vmem((16, 8, 4, 128), F32),
            vmem((16, 8, 4, 128), F32),
            vmem((SWEEPS, 3, 10, 16, 256), F32),
            vmem((SWEEPS, 3, 10, 16, 256), F32),
            vmem((8, 16, 256), F32),
            vmem((8, 16, 256), F32),
            vmem((6, 8, 16, 256), F32),
            vmem((6, 8, 16, 256), F32),
            vmem((3, 8, 16, 256), F32),
            vmem((3, 8, 16, 256), F32),
            vmem((2, SWEEPS, 2, 3, 8, 256), F32),
            vmem((2, SWEEPS, 2, 3, 8, 256), F32),
            vmem((2, 2, 8, 256), F32),
            pltpu.SemaphoreType.DMA((12,)),
            pltpu.SemaphoreType.DMA((4,)),
            pltpu.SemaphoreType.DMA((4,)),
            pltpu.SemaphoreType.DMA((2, SWEEPS, 4)),
            pltpu.SemaphoreType.DMA((2, SWEEPS, 4)),
        ],
        compiler_params=pltpu.CompilerParams(
            collective_id=0, has_side_effects=True, vmem_limit_bytes=63 * 2**20
        ),
        name="overset",
    )(*args)


def solution(mesh):
    return jax.shard_map(
        body,
        mesh=mesh,
        in_specs=(
            P(None, "grp", "sub", None),
            P(None, "grp", "sub", None),
            P(None, "grp", "sub", None),
            P(None, "grp", "sub", None),
            P("grp", "sub", None),
            P("grp", "sub", None),
            P(("grp", "sub"), None, None),
            P(("grp", "sub"), None, None, None),
            P(("grp", "sub"), None, None),
            P(("grp", "sub"), None, None, None),
            P(("grp", "sub"), None, None),
            P(("grp", "sub"), None, None),
        ),
        out_specs=(P(None, "grp", "sub", None), P(None, "grp", "sub", None)),
        check_vma=False,
    )
```

```python
import functools

import jax
import jax.numpy as jnp
from jax import lax
from jax.experimental import pallas as pl
from jax.experimental.pallas import tpu as pltpu
from jax.sharding import PartitionSpec as P

BF = jnp.bfloat16
F32 = jnp.float32
F8 = jnp.float8_e4m3fn
REACH = 1024.0
TINY = 1e-30
MESH = pl.DeviceIdType.MESH
SWEEPS = 4


def split(x):
    hi = x.astype(BF)
    lo = (x - hi.astype(F32)).astype(BF)
    return hi, lo


def iota(shape, dim):
    return lax.broadcasted_iota(jnp.int32, shape, dim)


def scales(peak):
    peak = jnp.maximum(jnp.max(jnp.max(peak, axis=0, keepdims=True), axis=1, keepdims=True), 1e-30)
    return REACH / peak, peak * (1.0 / REACH)


def build_table(field, high, low, low8):
    peak = jnp.maximum(jnp.maximum(jnp.abs(field[0]), jnp.abs(field[1])), jnp.abs(field[2]))
    scale, back = scales(peak.reshape(128, 256))
    for c in range(3):
        here = field[c].reshape(128, 256) * scale
        for zc, x in enumerate((here, pltpu.roll(here, 255, 1))):
            hi, lo = split(x)
            for xx in range(8):
                at = xx * 96 + zc * 48 + c * 16
                high[at : at + 16, :] = hi[xx * 16 : xx * 16 + 16]
                low[at : at + 16, :] = lo[xx * 16 : xx * 16 + 16]
    low8[...] = low[...].astype(F8)
    return back


def interpolate_tile(t, cells, weights, out, high, low8, back):
    z_iota = iota((256, 128), 0).astype(F32).astype(BF)
    y_iota = iota((16, 128), 0)
    tile = cells[0, pl.ds(pl.multiple_of(t * 8, 8), 8), :]
    z_tile = (tile & 255).astype(F32).astype(BF)
    y_tile = (tile >> 8) & 15
    x_tile = tile >> 12
    for pair in range(4):
        hot = [
            jnp.where(z_iota == z_tile[s : s + 1, :], jnp.ones((), BF), jnp.zeros((), BF))
            for s in (2 * pair, 2 * pair + 1)
        ]
        hot = jnp.concatenate(hot, axis=1)
        hot8 = hot.astype(F8)
        got = jnp.dot(high[...], hot, preferred_element_type=F32)
        got = got + jnp.dot(low8[...], hot8, preferred_element_type=F32)
        for half in range(2):
            s = 2 * pair + half
            w = weights[0, t * 8 + s]
            y_row = y_tile[s : s + 1, :]
            x_row = jnp.broadcast_to(x_tile[s : s + 1, :], (16, 128))
            y_here = y_iota == y_row
            y_next = y_iota == y_row + 1
            by_y = {}
            for a in range(2):
                for zc in range(2):
                    k = 4 * a + zc
                    by_y[a, zc] = jnp.where(
                        y_here, w[k : k + 1, :], jnp.where(y_next, w[k + 2 : k + 3, :], 0.0)
                    )
            acc = [None] * 3
            before = None
            for xx in range(8):
                here = x_row == xx if xx < 7 else None
                for zc in range(2):
                    coef = None
                    if before is not None:
                        coef = jnp.where(before, by_y[1, zc], 0.0)
                    if here is not None:
                        coef = jnp.where(here, by_y[0, zc], 0.0 if coef is None else coef)
                    for c in range(3):
                        at = xx * 96 + zc * 48 + c * 16
                        term = coef * got[at : at + 16, half * 128 : half * 128 + 128]
                        acc[c] = term if acc[c] is None else acc[c] + term
                before = here
            for c in range(3):
                out[t // 2, (t % 2) * 8 + s, c, :] = jnp.sum(acc[c], axis=0) * back[0]


def interpolate(field, cells, weights, sent, tables, ready, beside):
    high, low, low8 = tables
    back = build_table(field, high, low, low8)
    ready()

    def step(i, carry):
        beside(i)
        interpolate_tile(i, cells, weights, sent, high, low8, back)
        return carry

    lax.fori_loop(0, 16, step, 0)


class Exchange:
    def __init__(self, sent, held, came, sems, g, s, turn):
        self.sent, self.held, self.came, self.sems, self.g, self.s = sent, held, came, sems, g, s
        self.turn = turn

    def across(self, offset):
        peer = (self.g + offset) % 8
        return pltpu.make_async_remote_copy(
            src_ref=self.sent.at[peer],
            dst_ref=self.held.at[self.g],
            send_sem=self.sems.at[0],
            recv_sem=self.sems.at[1],
            device_id=(peer, self.s),
            device_id_type=MESH,
        )

    def along(self, offset):
        peer = (self.s + offset) % 16
        return pltpu.make_async_remote_copy(
            src_ref=self.held.at[:, peer],
            dst_ref=self.came.at[self.s],
            send_sem=self.sems.at[2],
            recv_sem=self.sems.at[3],
            device_id=(self.g, peer),
            device_id_type=MESH,
        )

    def all_across(self):
        return pltpu.make_async_remote_copy(
            src_ref=self.sent.at[pl.ds(0, 7)],
            dst_ref=self.held.at[pl.ds(0, 7)],
            send_sem=self.sems.at[0],
            recv_sem=self.sems.at[1],
            device_id=((self.g + 1) % 8, self.s),
            device_id_type=MESH,
        )

    def all_along(self):
        return pltpu.make_async_remote_copy(
            src_ref=self.came.at[pl.ds(0, 15)],
            dst_ref=self.came.at[pl.ds(0, 15)],
            send_sem=self.sems.at[2],
            recv_sem=self.sems.at[3],
            device_id=(self.g, (self.s + 1) % 16),
            device_id_type=MESH,
        )

    def first_hop(self):
        for offset in (4, 3, 5, 2, 6, 1, 7):
            self.across(offset).start()
        self.held[self.g] = self.sent[self.g]

    def second_hop(self, i):
        @pl.when(i == self.turn)
        def _():
            self.all_across().wait_recv()
            for offset in range(1, 16):
                self.along(offset).start()
            self.came[self.s] = self.held[:, self.s]

    def arrive(self):
        self.all_along().wait_recv()

    def finish(self):
        self.all_across().wait_send()
        self.all_along().wait_send()


def overwrite(field, receptors, got, start, frozen, total, beside):
    z_iota = iota((256, 128), 0).astype(F32).astype(BF)
    r_iota = iota((128, 128), 0).astype(F32).astype(BF)
    row = iota((4, 128), 0)
    peak = jnp.zeros((4, 128), F32)
    for p in range(16):
        peak = jnp.maximum(peak, jnp.max(jnp.abs(got[p]), axis=0))
    scale, back = scales(jnp.where(row < 3, peak, 0.0))
    one = jnp.ones((), BF)
    zero = jnp.zeros((), BF)
    total[...] = jnp.zeros_like(total)

    def step(i, carry):
        beside(i)
        tile = receptors[0, pl.ds(pl.multiple_of(i * 8, 8), 8), :]
        z_tile = (tile & 255).astype(F32).astype(BF)
        r_tile = (tile >> 8).astype(F32).astype(BF)
        for half in range(2):
            hots = []
            highs = []
            lows = []
            for s in range(4 * half, 4 * half + 4):
                hots.append(jnp.where(z_iota == z_tile[s : s + 1, :], one, zero))
                mine = r_iota == r_tile[s : s + 1, :]
                hi, lo = split(got[(i % 2) * 8 + s, i // 2] * scale)
                hi = hi.astype(F32)
                hi = jnp.where((hi == 0.0) & (row == 0), TINY, hi).astype(BF)
                for rows, part in ((highs, hi), (lows, lo)):
                    picked = [jnp.where(mine, part[c : c + 1, :], zero) for c in range(3)]
                    rows.append(jnp.concatenate(picked, axis=0))
            hot = jnp.concatenate(hots, axis=1)
            hot8 = hot.astype(F8)
            over_slots = (((1,), (1,)), ((), ()))
            total[...] += lax.dot_general(
                jnp.concatenate(highs, axis=1), hot, over_slots, preferred_element_type=F32
            ) + lax.dot_general(
                jnp.concatenate(lows, axis=1).astype(F8),
                hot8,
                over_slots,
                preferred_element_type=F32,
            )
        return carry

    lax.fori_loop(0, 16, step, 0)
    mask = total[0:128, :] != 0.0
    frozen[...] = jnp.where(mask, 1.0, 0.0).reshape(8, 16, 256)
    for c in range(3):
        value = total[c * 128 : c * 128 + 128, :]
        if c == 0:
            value = jnp.where(jnp.abs(value) < 2.0 * TINY, 0.0, value)
        old = field[c].reshape(128, 256)
        start[c, 1:9] = jnp.where(mask, value * back, old).reshape(8, 16, 256)


def halo_copies(grid, k, velocity, edge, halo, send_sems, recv_sems, g, s):
    north, south = (s + 1) % 16, (s + 15) % 16
    plan = [
        (edge.at[grid, k, 0], halo.at[grid, k, 0], (g, north)),
        (edge.at[grid, k, 1], halo.at[grid, k, 1], (g, south)),
    ]
    if grid == 0:
        plan += [
            (velocity.at[k, :, 8], velocity.at[k, :, 0], ((g + 1) % 8, s)),
            (velocity.at[k, :, 1], velocity.at[k, :, 9], ((g + 7) % 8, s)),
        ]
    return [
        pltpu.make_async_remote_copy(
            src_ref=source,
            dst_ref=target,
            send_sem=send_sems.at[grid, k, n],
            recv_sem=recv_sems.at[grid, k, n],
            device_id=device,
            device_id_type=MESH,
        )
        for n, (source, target, device) in enumerate(plan)
    ]


def fill_edges(grid, k, velocity, edge):
    for c in range(3):
        edge[grid, k, 0, c] = velocity[k, c, 1:9, 15, :]
        edge[grid, k, 1, c] = velocity[k, c, 1:9, 0, :]


def shifted(plane, low, high):
    y = iota((16, 256), 0)
    after_y = jnp.where(y == 15, high, pltpu.roll(plane, 15, 0))
    before_y = jnp.where(y == 0, low, pltpu.roll(plane, 1, 0))
    return after_y, before_y, pltpu.roll(plane, 255, 1), pltpu.roll(plane, 1, 1)


def assemble(grid, velocity, halo, source, inertia, frozen, coef, rhs, rim, g, s):
    y = iota((16, 256), 0)
    z = iota((16, 256), 1)
    y_low = jnp.where(s > 0, 1.0, 0.0)
    y_high = jnp.where(s < 15, 1.0, 0.0)

    def face(middle, other, sign):
        return 1.0 + jnp.maximum(sign * (middle + other), 0.0)

    def step(x, carry):
        u, v, w = (velocity[0, c, x + 1] for c in range(3))
        if grid == 0:
            x_low = jnp.where((x > 0) | (g > 0), 1.0, 0.0)
            x_high = jnp.where((x < 7) | (g < 7), 1.0, 0.0)
        else:
            x_low = jnp.where(x > 0, 1.0, 0.0)
            x_high = jnp.where(x < 7, 1.0, 0.0)
        low = halo[grid, 0, 0, 1, pl.ds(x, 1), :] * y_low
        high = halo[grid, 0, 1, 1, pl.ds(x, 1), :] * y_high
        v_after, v_before, _, _ = shifted(v, low, high)
        w_after = jnp.where(z == 255, 0.0, pltpu.roll(w, 255, 1))
        w_before = jnp.where(z == 0, 0.0, pltpu.roll(w, 1, 1))
        faces = [
            face(u, velocity[0, 0, x + 2] * x_high, -0.5),
            face(u, velocity[0, 0, x] * x_low, 0.5),
            face(v, v_after, -0.5),
            face(v, v_before, 0.5),
            face(w, w_after, -0.5),
            face(w, w_before, 0.5),
        ]
        weight = inertia[x]
        diagonal = weight
        for f in faces:
            diagonal = diagonal + f
        inverse = 1.0 / diagonal
        stuck = frozen[x] > 0.5
        live = jnp.where(stuck, 0.0, inverse)
        faces = [f * live for f in faces]
        coef[0, x] = faces[0] * x_high
        coef[1, x] = faces[1] * x_low
        coef[2, x] = faces[2]
        coef[3, x] = faces[3]
        coef[4, x] = jnp.where(z == 255, 0.0, faces[4])
        coef[5, x] = jnp.where(z == 0, 0.0, faces[5])
        for c, start in enumerate((u, v, w)):
            right = (source[c, x] + weight * start) * inverse
            rhs[c, x] = jnp.where(stuck, start, right)
        return carry

    lax.fori_loop(0, 8, step, 0, unroll=4)
    rim[grid, 0] = coef[3, :, 0, :] * y_low
    rim[grid, 1] = coef[2, :, 15, :] * y_high
    coef[3, :, 0, :] = jnp.zeros((8, 256), F32)
    coef[2, :, 15, :] = jnp.zeros((8, 256), F32)


def inner(now, coef, rhs, after):
    for x in range(8):
        for c in range(3):
            plane = now[c, x + 1]
            total = rhs[c, x]
            if x < 7:
                total = total + coef[0, x] * now[c, x + 2]
            if x > 0:
                total = total + coef[1, x] * now[c, x]
            total = total + coef[2, x] * pltpu.roll(plane, 15, 0)
            total = total + coef[3, x] * pltpu.roll(plane, 1, 0)
            total = total + coef[4, x] * pltpu.roll(plane, 255, 1)
            total = total + coef[5, x] * pltpu.roll(plane, 1, 1)
            after[c, x] = total


def outer(grid, k, now, halo, coef, rim, after, edge):
    for c in range(3):
        if grid == 0:
            after[c, 0] = after[c, 0] + coef[1, 0] * now[c, 0]
            after[c, 7] = after[c, 7] + coef[0, 7] * now[c, 9]
        low = after[c, :, 0, :] + rim[grid, 0] * halo[grid, k, 0, c]
        high = after[c, :, 15, :] + rim[grid, 1] * halo[grid, k, 1, c]
        after[c, :, 0, :] = low
        after[c, :, 15, :] = high
        if k < SWEEPS - 1:
            edge[grid, k + 1, 0, c] = high
            edge[grid, k + 1, 1, c] = low


def kernel(*refs):
    (
        bg_vel_hbm, nb_vel_hbm, bg_source_hbm, nb_source_hbm, bg_inertia_hbm, nb_inertia_hbm,
        bg_cells_hbm, bg_weights_hbm, nb_cells_hbm, nb_weights_hbm, nb_rec_hbm, bg_rec_hbm,
        bg_out, nb_out,
        bg_vel, nb_vel, bg_source, nb_source, bg_inertia, nb_inertia,
        bg_cells, bg_weights, nb_cells, nb_weights, nb_rec, bg_rec,
        high, low, low8, total,
        bg_sent, nb_sent, bg_held, nb_held, to_near, to_back, bg_run, nb_run,
        bg_frozen, nb_frozen, bg_coef, nb_coef, bg_rhs, nb_rhs, edge, halo, rim,
        load_sems, near_sems, back_sems, send_sems, recv_sems,
    ) = refs
    g = lax.axis_index("grp")
    s = lax.axis_index("sub")

    hbm = refs[:12]
    vmem = refs[14:26]
    loads = [
        pltpu.make_async_copy(hbm[n], vmem[n], load_sems.at[n]) for n in range(12)
    ]
    for n in (0, 6, 7):
        loads[n].start()

    barrier = pltpu.get_barrier_semaphore()

    for c in range(3):
        for end in (0, 9):
            nb_run[0, c, end] = jnp.zeros((16, 256), F32)
            for k in range(SWEEPS):
                bg_run[k, c, end] = jnp.zeros((16, 256), F32)
    halo[...] = jnp.zeros_like(halo)
    for offset in range(1, 8):
        pl.semaphore_signal(
            barrier, inc=1, device_id=((g + offset) % 8, s), device_id_type=MESH
        )
    for offset in range(1, 16):
        pl.semaphore_signal(
            barrier, inc=1, device_id=(g, (s + offset) % 16), device_id_type=MESH
        )

    near = Exchange(bg_sent, bg_held, to_near, near_sems, g, s, 7)
    back = Exchange(nb_sent, nb_held, to_back, back_sems, g, s, 5)
    def bg_ready():
        for n in (6, 7):
            loads[n].wait()
        for n in (1, 8, 9, 10, 11, 2, 3, 4, 5):
            loads[n].start()

    loads[0].wait()
    interpolate(bg_vel, bg_cells, bg_weights, bg_sent, (high, low, low8), bg_ready, lambda i: None)
    for n in (1, 8, 9):
        loads[n].wait()
    pl.semaphore_wait(barrier, 22)
    near.first_hop()
    interpolate(nb_vel, nb_cells, nb_weights, nb_sent, (high, low, low8), lambda: None, near.second_hop)
    for n in (10, 11, 2, 3, 4, 5):
        loads[n].wait()
    back.first_hop()
    near.arrive()
    overwrite(nb_vel, nb_rec, to_near, nb_run.at[0], nb_frozen, total, back.second_hop)

    goes = (s < 15, s > 0, g < 7, g > 0)
    comes = (s > 0, s < 15, g > 0, g < 7)
    copies = []

    def each(conditions, new, act):
        for condition, copy in zip(conditions, new):
            pl.when(condition)(functools.partial(act, copy))

    def exchange(grid, k, velocity):
        new = halo_copies(grid, k, velocity, edge, halo, send_sems, recv_sems, g, s)
        each(goes, new, lambda copy: copy.start())
        copies.append(new)
        return new

    fill_edges(1, 0, nb_run, edge)
    nb_moving = exchange(1, 0, nb_run)
    back.arrive()
    overwrite(bg_vel, bg_rec, to_back, bg_run.at[0], bg_frozen, total, lambda i: None)
    fill_edges(0, 0, bg_run, edge)
    moving = [exchange(0, 0, bg_run), nb_moving]

    runs = (bg_run, nb_run)
    outs = (bg_out, nb_out)
    coefs = (bg_coef, nb_coef)
    sides = (bg_rhs, nb_rhs)
    fields = ((bg_source, bg_inertia, bg_frozen), (nb_source, nb_inertia, nb_frozen))
    for k in range(SWEEPS):
        for grid in (1, 0):
            run, coef, rhs = runs[grid], coefs[grid], sides[grid]
            now = run.at[k]
            after = run.at[k + 1, :, pl.ds(1, 8)] if k < SWEEPS - 1 else outs[grid]
            if k == 0:
                each(comes, moving[grid], lambda copy: copy.wait_recv())
                assemble(grid, run, halo, *fields[grid], coef, rhs, rim, g, s)
            inner(now, coef, rhs, after)
            if k > 0:
                each(comes, moving[grid], lambda copy: copy.wait_recv())
            outer(grid, k, now, halo, coef, rim, after, edge)
            if k < SWEEPS - 1:
                moving[grid] = exchange(grid, k + 1, run)

    near.finish()
    back.finish()
    for new in copies:
        each(goes, new, lambda copy: copy.wait_send())


def body(*args):
    out = jax.ShapeDtypeStruct((3, 8, 16, 256), F32)
    vmem = pltpu.VMEM
    return pl.pallas_call(
        kernel,
        out_shape=(out, out),
        in_specs=[pl.BlockSpec(memory_space=pl.ANY)] * 12,
        out_specs=[pl.BlockSpec(memory_space=vmem)] * 2,
        scratch_shapes=[vmem(a.shape, a.dtype) for a in args]
        + [
            vmem((768, 256), BF),
            vmem((768, 256), BF),
            vmem((768, 256), F8),
            vmem((384, 256), F32),
            vmem((8, 16, 4, 128), F32),
            vmem((8, 16, 4, 128), F32),
            vmem((8, 16, 4, 128), F32),
            vmem((8, 16, 4, 128), F32),
            vmem((16, 8, 4, 128), F32),
            vmem((16, 8, 4, 128), F32),
            vmem((SWEEPS, 3, 10, 16, 256), F32),
            vmem((SWEEPS, 3, 10, 16, 256), F32),
            vmem((8, 16, 256), F32),
            vmem((8, 16, 256), F32),
            vmem((6, 8, 16, 256), F32),
            vmem((6, 8, 16, 256), F32),
            vmem((3, 8, 16, 256), F32),
            vmem((3, 8, 16, 256), F32),
            vmem((2, SWEEPS, 2, 3, 8, 256), F32),
            vmem((2, SWEEPS, 2, 3, 8, 256), F32),
            vmem((2, 2, 8, 256), F32),
            pltpu.SemaphoreType.DMA((12,)),
            pltpu.SemaphoreType.DMA((4,)),
            pltpu.SemaphoreType.DMA((4,)),
            pltpu.SemaphoreType.DMA((2, SWEEPS, 4)),
            pltpu.SemaphoreType.DMA((2, SWEEPS, 4)),
        ],
        compiler_params=pltpu.CompilerParams(
            collective_id=0, has_side_effects=True, vmem_limit_bytes=63 * 2**20
        ),
        name="overset",
    )(*args)


def solution(mesh):
    return jax.shard_map(
        body,
        mesh=mesh,
        in_specs=(
            P(None, "grp", "sub", None),
            P(None, "grp", "sub", None),
            P(None, "grp", "sub", None),
            P(None, "grp", "sub", None),
            P("grp", "sub", None),
            P("grp", "sub", None),
            P(("grp", "sub"), None, None),
            P(("grp", "sub"), None, None, None),
            P(("grp", "sub"), None, None),
            P(("grp", "sub"), None, None, None),
            P(("grp", "sub"), None, None),
            P(("grp", "sub"), None, None),
        ),
        out_specs=(P(None, "grp", "sub", None), P(None, "grp", "sub", None)),
        check_vma=False,
    )
```
